256 devices in a mesh: lon: 32 (over z, y_lo, core), lat: 8 (over x, y_hi).
Axes of the slice: x: 4, y: 4 (y_hi: 2, y_lo: 2; y = y_hi * 2 + y_lo), z: 8, core: 2. Of those that a mesh axis runs over, the one named last changes fastest.
Arguments:
- adjoint: float32 [4, 4, 4320, 1024], P(None, None, 'lon', 'lat'), may hold values from -6 to 6
- land: int32 [4320, 1024], P('lon', 'lat'), may hold values from 0 to 1, as said below
- diffusivity: float32 [2, 4320, 1024], P(None, 'lon', 'lat'), may hold values from 0.01 to 0.2
- cutoff: int32 [128], replicated, may hold values from 270 to 2160
Outputs:
- adjoint_in: float32 [4, 4, 4320, 1024], P(None, None, 'lon', 'lat')
The draws below stay inside these ranges and needn't reach their ends.
Inputs may be any that keep to these rules, and one draw needn't show every extreme that they name: In each of the first 64 and the last 64 latitude rows the land cells form one run of consecutive longitudes around the circle, of 270 to 1080 cells; the rest of that row is ocean.
All inputs are finite; a program needn't handle non-finite values.
Results may differ from the reference program's by a relative error of at most 0.0009.
Values may be sent and summed in bfloat16 or wider, within the bound.
No kernel may reach another device: no remote copies, remote signals or barrier semaphores. Data moves between devices by JAX's collectives and lax.ppermute only.
A program may use at most 128 MiB of HBM per device.

```python
import math
import jax
import jax.numpy as jnp
from jax import lax

NLON = 4320
LEV = 4
PROWS = 64
NLAT = 1024


def zonal_waves(key, levels, amplitude_lo, amplitude_hi):
    key_mean, key_waves, key_phase, key_amp = jax.random.split(key, 4)
    longitudes = jnp.arange(NLON, dtype=jnp.int32).reshape(1, 1, NLON, 1)
    smooth = jax.random.uniform(key_mean, (4, levels, 1, NLAT), jnp.float32, -0.75, 0.75)
    top_wave = max(2, NLON // 16)
    for term in range(3):
        wave_key = jax.random.fold_in(key_waves, term)
        phase_key = jax.random.fold_in(key_phase, term)
        amp_key = jax.random.fold_in(key_amp, term)
        wavenumber = jax.random.randint(wave_key, (4, levels, 1, NLAT), 1, top_wave, dtype=jnp.int32)
        phase_index = wavenumber * longitudes % NLON
        offset = jax.random.uniform(phase_key, (4, levels, 1, NLAT), jnp.float32, -math.pi, math.pi)
        amplitude = jax.random.uniform(amp_key, (4, levels, 1, NLAT), jnp.float32, amplitude_lo, amplitude_hi)
        angle = phase_index.astype(jnp.float32) * (2.0 * math.pi / NLON) + offset
        smooth = smooth + amplitude * jnp.cos(angle)
    return smooth


def draw_adjoint(key, part):
    key = jax.random.fold_in(key, 11)
    key_noise, key_smooth = jax.random.split(key, 2)
    shape = (4, LEV, NLON, NLAT)
    noise = jax.random.normal(key_noise, shape, jnp.float32)
    smooth = zonal_waves(key_smooth, LEV, 0.4, 0.8)
    return jnp.clip(noise + smooth, -6.0, 6.0).astype(jnp.float32)


def draw_land(key, part):
    key = jax.random.fold_in(key, 12)
    key_base, key_start, key_length = jax.random.split(key, 3)
    base = (jax.random.randint(key_base, (NLON, NLAT), 0, 5, dtype=jnp.int32) < 4).astype(jnp.int32)
    starts = jax.random.randint(key_start, (NLAT,), 0, NLON, dtype=jnp.int32)
    lengths = jax.random.randint(key_length, (NLAT,), NLON // 16, NLON // 4 + 1, dtype=jnp.int32)
    longitudes = jnp.arange(NLON, dtype=jnp.int32)[:, None]
    in_run = (longitudes - starts[None, :]) % NLON < lengths[None, :]
    latitudes = jnp.arange(NLAT, dtype=jnp.int32)[None, :]
    polar = jnp.logical_or(latitudes < PROWS, latitudes >= NLAT - PROWS)
    polar_land = jnp.where(in_run, 0, 1).astype(jnp.int32)
    return jnp.where(polar, polar_land, base).astype(jnp.int32)


def with_ends(array, rng, low, largest):
    longest = array.shape.index(max(array.shape))
    spots = []
    for shift in (0, 1):
        where = [jax.random.randint(jax.random.fold_in(rng, axis), (), 0, length) for axis, length in enumerate(array.shape)]
        where[longest] = (where[longest] + shift) % array.shape[longest]
        spots.append(tuple(where))
    return array.at[spots[0]].set(low).at[spots[1]].set(largest)


def shard_levels(key, dims, pieces, smallest, high):
    def one(position, parts):
        draws = jax.random.uniform(jax.random.fold_in(jax.random.fold_in(key, 6), position), (parts,), jnp.float32, smallest / len(pieces), high / len(pieces))
        return jnp.repeat(jnp.exp(draws), dims[position] // parts).reshape((-1,) + (1,) * (len(dims) - position - 1))

    loudness = one(*pieces[0])
    for cut in pieces[1:]:
        loudness = loudness * one(*cut)
    return loudness


def setup_inputs(seed: int = 0) -> dict:
    key_of = jax.random.split(jax.random.key(seed), 5)
    adjoint = draw_adjoint(jax.random.fold_in(key_of[4], 71), 0)
    land = draw_land(jax.random.fold_in(key_of[4], 71), 0)
    diffusivity = jnp.clip(jnp.exp(math.log(0.2) - 2.9957323 * jax.random.uniform(key_of[2], (2, NLON, NLAT), jnp.float32) ** shard_levels(key_of[2], (2, NLON, NLAT), ((1, 32), (2, 8)), -0.2, 0.2)), 0.01, 0.2)
    cutoff = with_ends(jax.random.randint(key_of[3], (2 * PROWS,), NLON // 16, NLON // 2 + 1), jax.random.fold_in(key_of[3], 1), NLON // 16, (NLON // 2 + 1) - 1).astype(jnp.int32)
    return dict(adjoint=adjoint, land=land, diffusivity=diffusivity, cutoff=cutoff)


PRESSURE = 0.3
ALPHA_T = 1.0
BETA_S = 0.8


def diffuse(padded, mask_pad, kappa_pad):
    extent = padded.shape[-2] - 2
    height = padded.shape[-1] - 2
    centre = padded[..., 1:-1, 1:-1]
    mask_centre = mask_pad[1:-1, 1:-1]
    kappa_centre = kappa_pad[1:-1, 1:-1]
    accumulated = jnp.zeros_like(centre)
    for offset_a, offset_b in ((0, 1), (2, 1), (1, 0), (1, 2)):
        neighbour = padded[..., offset_a:offset_a + extent, offset_b:offset_b + height]
        face_weight = 0.5 * (kappa_centre + kappa_pad[offset_a:offset_a + extent, offset_b:offset_b + height]) * mask_centre * mask_pad[offset_a:offset_a + extent, offset_b:offset_b + height]
        accumulated = accumulated + face_weight * (neighbour - centre)
    return accumulated


def adjoint_step(extended, levels):
    extent = extended.shape[1] - 2
    height = extended.shape[2] - 2
    fields_pad = extended[:4 * levels].reshape(4, levels, extent + 2, height + 2)
    mask_pad = extended[4 * levels]
    kappa_mom = extended[4 * levels + 1]
    kappa_trc = extended[4 * levels + 2]
    zonal_pad = fields_pad[0]
    merid_pad = fields_pad[1]
    temper_pad = fields_pad[2]
    saline_pad = fields_pad[3]
    zonal_c = zonal_pad[:, 1:-1, 1:-1]
    merid_c = merid_pad[:, 1:-1, 1:-1]
    mask_centre = mask_pad[1:-1, 1:-1]
    mask_east = mask_pad[2:, 1:-1]
    mask_north = mask_pad[1:-1, 2:]
    zonal_west = zonal_pad[:, :-2, 1:-1]
    merid_south = merid_pad[:, 1:-1, :-2]
    adjoint_rho = PRESSURE * (mask_east * zonal_c + mask_north * merid_c) - PRESSURE * mask_centre * (zonal_west + merid_south)
    zonal_out = zonal_c + diffuse(zonal_pad, mask_pad, kappa_mom)
    merid_out = merid_c + diffuse(merid_pad, mask_pad, kappa_mom)
    temper_out = temper_pad[:, 1:-1, 1:-1] + diffuse(temper_pad, mask_pad, kappa_trc) - ALPHA_T * adjoint_rho
    saline_out = saline_pad[:, 1:-1, 1:-1] + diffuse(saline_pad, mask_pad, kappa_trc) + BETA_S * adjoint_rho
    return jnp.stack([zonal_out, merid_out, temper_out, saline_out], 0)


def back_product(coefs, table):
    return lax.dot_general(coefs, table, (((1,), (1,)), ((), ())), preferred_element_type=jnp.float32)


def highpass(row_block, row_cuts):
    count_lon = row_block.shape[1]
    halfway = count_lon // 2
    per_block = halfway // 4
    positions = jnp.arange(count_lon, dtype=jnp.int32)
    result = jnp.zeros((row_block.shape[0], count_lon), jnp.float32)
    cut_float = row_cuts.astype(jnp.float32)[:, None]
    for block_number in range(4):
        wavenumbers = jnp.arange(per_block, dtype=jnp.int32) + block_number * per_block + 1
        phase_index = (positions[:, None] * wavenumbers[None, :]) % count_lon
        angles = phase_index.astype(jnp.float32) * (2.0 * math.pi / count_lon)
        cosine = jnp.cos(angles).astype(jnp.bfloat16)
        sine_table = jnp.sin(angles).astype(jnp.bfloat16)
        along_cos = jnp.dot(row_block, cosine, preferred_element_type=jnp.float32)
        along_sin = jnp.dot(row_block, sine_table, preferred_element_type=jnp.float32)
        wave_float = wavenumbers.astype(jnp.float32)[None, :]
        damping = jnp.maximum(0.0, 1.0 - (cut_float / wave_float) ** 2)
        weights = jnp.where(wavenumbers == halfway, 1.0 / count_lon, 2.0 / count_lon).astype(jnp.float32)[None, :]
        coef_cos = (along_cos * damping * weights).astype(jnp.bfloat16)
        coef_sin = (along_sin * damping * weights).astype(jnp.bfloat16)
        result = result + back_product(coef_cos, cosine)
        result = result + back_product(coef_sin, sine_table)
    return result


def reference(adjoint, land, diffusivity, cutoff):
    levels = adjoint.shape[1]
    mask_float = land.astype(jnp.float32)
    masked = adjoint * mask_float
    stacked = jnp.concatenate([masked.reshape(4 * levels, NLON, NLAT), mask_float[None], diffusivity], 0)
    stacked = jnp.concatenate([stacked[:, -1:, :], stacked, stacked[:, :1, :]], 1)
    stacked = jnp.pad(stacked, ((0, 0), (0, 0), (1, 1)))
    middle = adjoint_step(stacked, levels)
    momentum = middle[:2]
    for band in range(2):
        first_row = 0 if band == 0 else NLAT - PROWS
        band_block = momentum[:, :, :, first_row:first_row + PROWS]
        flat_rows = jnp.transpose(band_block, (0, 1, 3, 2)).reshape(2 * levels * PROWS, NLON).astype(jnp.bfloat16)
        row_cuts = jnp.tile(cutoff[band * PROWS:(band + 1) * PROWS], 2 * levels)
        removed = highpass(flat_rows, row_cuts).reshape(2, levels, PROWS, NLON)
        removed = jnp.transpose(removed, (0, 1, 3, 2))
        momentum = momentum.at[:, :, :, first_row:first_row + PROWS].set(band_block - removed)
    return jnp.concatenate([momentum, middle[2:]], 0)
```

```python
import math

import jax
import jax.numpy as jnp
import numpy as np
from jax import lax
from jax.experimental import pallas as pl
from jax.experimental.pallas import tpu as pltpu
from jax.sharding import PartitionSpec as P

PROWS = 64
PRESSURE = 0.3
ALPHA_T = 1.0
BETA_S = 0.8

RING = 32
COLS = 135
NLON = RING * COLS
INV = 23
CRT_RING = 3105
CRT_COLS = 1216
WAVES = 68
ROWS = 16
CHUNK = 24

MAIN = [lane + 1 for lane in range(128)]
EXTRA = [0] + list(range(129, 135))

F32 = jnp.float32
BF16 = jnp.bfloat16


def tables():
    order = np.array(MAIN + EXTRA + [0] * 121)
    used = np.array([1.0] * 135 + [0.0] * 121)
    waves = np.arange(WAVES)
    angle = 2.0 * math.pi * ((38 * order[:, None] * waves[None, :]) % COLS) / COLS
    forward = np.zeros((256, 256))
    forward[:, :WAVES] = np.cos(angle) * used[:, None]
    forward[:, 128 : 128 + WAVES] = -np.sin(angle) * used[:, None]
    weight = np.where(waves == 0, 1.0, 2.0) / NLON
    backward = forward.copy().T
    backward[:WAVES] *= NLON * weight[:, None]
    backward[128 : 128 + WAVES] *= NLON * weight[:, None]
    inverse_square = np.ones((RING, 128))
    for place in range(RING):
        kappa = int(format(place, "05b")[::-1], 2)
        ring_wave = 7 * kappa % RING
        k = (CRT_RING * ring_wave + CRT_COLS * waves) % NLON
        k = np.minimum(k, NLON - k)
        inverse_square[place, :WAVES] = np.where(k == 0, 1e6, 1.0 / np.maximum(k, 1) ** 2)
    return (
        jnp.asarray(forward, BF16),
        jnp.asarray(backward, BF16),
        jnp.asarray(inverse_square, F32),
    )


def turn(value, shift):
    size = value.shape[-1]
    shift %= size
    return value if shift == 0 else pltpu.roll(value, shift, value.ndim - 1)


def lanes(shape):
    return lax.broadcasted_iota(jnp.int32, shape, len(shape) - 1)


def sublanes(shape):
    return lax.broadcasted_iota(jnp.int32, shape, len(shape) - 2)


def faces(mask, kappa, mask_near, kappa_near):
    return 0.5 * (kappa + kappa_near) * mask * mask_near


def pack_kernel(north_ref, adjoint_ref, land_ref, kappa_ref, out_ref, field, part):
    north = north_ref[0] != 0
    whole = (COLS, 128)
    low, high = pl.ds(7, COLS), pl.ds(9, COLS)
    centre = pl.ds(8, COLS)
    zero = jnp.zeros((8, 128), F32)
    for ref in (field,):
        ref[0:8] = zero
        ref[136:144] = zero
        ref[144:152] = zero
    lane = lanes(whole)
    mask = land_ref[...].astype(F32)
    kappa = kappa_ref[0]

    field[centre] = kappa
    kappa_west, kappa_east = field[low], field[high]
    field[centre] = mask
    mask_west, mask_east = field[low], field[high]
    west = faces(mask, kappa, mask_west, kappa_west)
    east = faces(mask, kappa, mask_east, kappa_east)
    up = faces(mask, kappa, jnp.where(lane == 127, 0.0, turn(mask, -1)), turn(kappa, -1))
    down = faces(mask, kappa, jnp.where(lane == 0, 0.0, turn(mask, 1)), turn(kappa, 1))
    own = 1.0 - (west + east + up + down)

    group = (8, 128)
    slot = sublanes(group)
    lane8 = lanes(group)
    edge_fixed = jnp.zeros(group, F32)
    for place, row in ((1, kappa[134:135]), (2, mask[134:135]), (4, kappa[0:1]), (5, mask[0:1])):
        edge_fixed = jnp.where(slot == place, row, edge_fixed)
    part[136:144] = zero
    for index in range(8):
        tilde = adjoint_ref[index // 4, index % 4] * mask
        field[centre] = tilde
        partial = (
            own * tilde
            + west * field[low]
            + east * field[high]
            + up * turn(tilde, -1)
            + down * turn(tilde, 1)
        )
        part[0:COLS] = partial
        turned = part[pl.ds(1, 128)].T
        chosen = jnp.where(north, turned[64:128], turned[0:64])
        others = jnp.where(slot == 0, partial[0:1], part[128:136])
        others = jnp.where(slot == 7, 0.0, others)
        edges = jnp.where(slot == 0, tilde[134:135], jnp.where(slot == 3, tilde[0:1], edge_fixed))
        others = jnp.where(north, turn(others, 64), others)
        edges = jnp.where(north, turn(edges, 64), edges)
        for quarter in range(4):
            place = 4 * index + quarter
            out_ref[place, 0:ROWS] = chosen[16 * quarter : 16 * quarter + 16].astype(BF16)
            out_ref[place, ROWS:CHUNK] = jnp.where(
                lane8 < 16, turn(others, -16 * quarter), turn(edges, 16 - 16 * quarter)
            ).astype(BF16)


def pack(north, adjoint, land, diffusivity):
    return pl.pallas_call(
        pack_kernel,
        grid=(1,),
        out_shape=jax.ShapeDtypeStruct((RING, CHUNK, 128), BF16),
        in_specs=[
            pl.BlockSpec(memory_space=pltpu.SMEM),
            pl.BlockSpec((2, 4, COLS, 128), lambda i: (0, 0, 0, 0)),
            pl.BlockSpec((COLS, 128), lambda i: (0, 0)),
            pl.BlockSpec((1, COLS, 128), lambda i: (0, 0, 0)),
        ],
        out_specs=pl.BlockSpec((RING, CHUNK, 128), lambda i: (0, 0, 0)),
        scratch_shapes=[pltpu.VMEM((152, 128), F32), pltpu.VMEM((144, 128), F32)],
        compiler_params=pltpu.CompilerParams(vmem_limit_bytes=24 * 2**20),
        name="pack",
    )(north, adjoint, land, diffusivity)


def times(re, im, angle_index, count, sign):
    eighth = 8 * angle_index // count if 8 * angle_index % count == 0 else None
    half = math.sqrt(0.5)
    if eighth == 0:
        return re, im
    if eighth == 2:
        return (-im, re) if sign > 0 else (im, -re)
    if eighth == 1:
        if sign > 0:
            return half * (re - im), half * (re + im)
        return half * (re + im), half * (im - re)
    if eighth == 3:
        if sign > 0:
            return -half * (re + im), half * (re - im)
        return half * (im - re), -half * (re + im)
    cos = math.cos(2.0 * math.pi * angle_index / count)
    sin = sign * math.sin(2.0 * math.pi * angle_index / count)
    return cos * re - sin * im, sin * re + cos * im


def fourier(values):
    half = RING // 2
    while half:
        for start in range(0, RING, 2 * half):
            for i in range(half):
                a, b = start + i, start + i + half
                (ar, ai), (br, bi) = values[a], values[b]
                values[a] = (ar + br, ai + bi)
                values[b] = times(ar - br, ai - bi, i, 2 * half, -1)
        half //= 2


def fourier_back(values):
    half = 1
    while half < RING:
        for start in range(0, RING, 2 * half):
            for i in range(half):
                a, b = start + i, start + i + half
                ar, ai = values[a]
                br, bi = times(*values[b], i, 2 * half, 1)
                values[a] = (ar + br, ai + bi)
                values[b] = (ar - br, ai - bi)
        half *= 2


def slot_shift(value, sign):
    slot = lanes(value.shape) % 8
    for bit in range(5):
        moved = turn(value, sign * 8 * 2**bit)
        picked = jnp.zeros(value.shape, jnp.bool_)
        for place, column in enumerate(EXTRA):
            if (INV * column % RING) >> bit & 1:
                picked = jnp.logical_or(picked, slot == place)
        value = jnp.where(picked, moved, value)
    return value


def filter_kernel(in_ref, square_ref, forward_ref, backward_ref, inverse_ref, out_ref, held, wave):
    tile = (ROWS, 128)
    spare = in_ref[:, ROWS:CHUNK, :].astype(F32).reshape(256, 128)
    spare = jnp.concatenate([spare[0:128].T[0:32], spare[128:256].T[0:32]], axis=1)
    others, edges = spare[0:16], spare[16:32]
    slot = lanes(others.shape) % 8
    beyond = turn(edges, -11)
    flux = (beyond - edges) * turn(0.5 * (beyond + edges), -1) * turn(beyond * edges, -2)
    others = others + jnp.where(slot == 6, turn(flux, 6), 0.0)
    others = others - jnp.where(slot == 0, turn(flux, 8), 0.0)
    others = slot_shift(others, 1)

    column = lanes(tile) + 1
    rows = [in_ref[INV * t % RING, 0:ROWS, :] for t in range(RING)]
    for bit in range(5):
        picked = (column >> bit) & 1 == 1
        rows = [jnp.where(picked, rows[(t - 2**bit) % RING], rows[t]) for t in range(RING)]
    for t in range(RING):
        place = INV * t % RING
        held[pl.ds(ROWS * t, ROWS), 0:128] = rows[t]
        side = others[:, 128 * (place // 16) : 128 * (place // 16) + 128]
        held[pl.ds(ROWS * t, ROWS), 128:256] = turn(side, -8 * (place % 16)).astype(BF16)

    wave[...] = jnp.dot(held[...], forward_ref[...], preferred_element_type=F32)
    for half in range(2):
        rows_of = [pl.ds(ROWS * t + 8 * half, 8) for t in range(RING)]
        values = [(wave[r, 0:128], wave[r, 128:256]) for r in rows_of]
        fourier(values)
        square = square_ref[8 * half : 8 * half + 8]
        for t in range(RING):
            keep = jnp.maximum(0.0, 1.0 - square * inverse_ref[t : t + 1]) * (1.0 / NLON)
            values[t] = (values[t][0] * keep, values[t][1] * keep)
        fourier_back(values)
        for t in range(RING):
            wave[rows_of[t], 0:128] = values[t][0]
            wave[rows_of[t], 128:256] = values[t][1]
    wave[...] = jnp.dot(wave[...].astype(BF16), backward_ref[...], preferred_element_type=F32)

    rows = [wave[pl.ds(ROWS * t, ROWS), 0:128] for t in range(RING)]
    for bit in range(5):
        picked = (column >> bit) & 1 == 1
        rows = [jnp.where(picked, rows[(t + 2**bit) % RING], rows[t]) for t in range(RING)]
    for d in range(RING):
        out_ref[d, 0:ROWS] = rows[7 * d % RING].astype(BF16)
    sides = [jnp.zeros(tile, F32), jnp.zeros(tile, F32)]
    for t in range(RING):
        place = INV * t % RING
        sides[place // 16] += turn(wave[pl.ds(ROWS * t, ROWS), 128:256], 8 * (place % 16))
    others = slot_shift(jnp.concatenate(sides, axis=1), -1)
    blank = jnp.zeros((112, 128), F32)
    for half in range(2):
        back = jnp.concatenate([others[:, 128 * half : 128 * half + 128], blank], axis=0).T
        out_ref[16 * half : 16 * half + 16, ROWS:CHUNK] = back.reshape(16, 8, 128).astype(BF16)


def filter_rows(chunks, square):
    forward, backward, inverse_square = tables()
    return pl.pallas_call(
        filter_kernel,
        out_shape=jax.ShapeDtypeStruct((RING, CHUNK, 128), BF16),
        in_specs=[pl.BlockSpec(memory_space=pltpu.VMEM)] * 5,
        out_specs=pl.BlockSpec(memory_space=pltpu.VMEM),
        scratch_shapes=[
            pltpu.VMEM((RING * ROWS, 256), BF16),
            pltpu.VMEM((RING * ROWS, 256), F32),
        ],
        compiler_params=pltpu.CompilerParams(vmem_limit_bytes=24 * 2**20),
        name="filter",
    )(chunks, square, forward, backward, inverse_square)


def edge_kernel(adjoint_ref, land_ref, kappa_ref, first_ref, last_ref, side_ref):
    whole = (COLS, 128)
    lane = lanes(whole)
    mask = land_ref[...].astype(F32)
    sides = jnp.zeros(whole, F32)
    first_ref[...] = jnp.zeros((24, 128), F32)
    last_ref[...] = jnp.zeros((24, 128), F32)
    for index in range(19):
        if index < 16:
            value = adjoint_ref[index // 4, index % 4] * mask
        elif index == 16:
            value = mask
        else:
            value = kappa_ref[index - 17]
        first_ref[index : index + 1] = value[0:1]
        last_ref[index : index + 1] = value[134:135]
        sides = jnp.where(lane // 2 == index, turn(value, 2 * index + 1), sides)
    side_ref[...] = sides


def edge(adjoint, land, diffusivity):
    return pl.pallas_call(
        edge_kernel,
        out_shape=(
            jax.ShapeDtypeStruct((24, 128), F32),
            jax.ShapeDtypeStruct((24, 128), F32),
            jax.ShapeDtypeStruct((COLS, 128), F32),
        ),
        in_specs=[pl.BlockSpec(memory_space=pltpu.VMEM)] * 3,
        out_specs=[pl.BlockSpec(memory_space=pltpu.VMEM)] * 3,
        compiler_params=pltpu.CompilerParams(vmem_limit_bytes=24 * 2**20),
        name="edge",
    )(adjoint, land, diffusivity)


def stencil_kernel(
    adjoint_ref, land_ref, kappa_ref, west_ref, east_ref, south_ref, north_ref, out_ref, field
):
    whole = (COLS, 128)
    lane = lanes(whole)
    centre, low, high = pl.ds(8, COLS), pl.ds(7, COLS), pl.ds(9, COLS)
    south_all, north_all = south_ref[...], north_ref[...]
    mask = land_ref[...].astype(F32)

    def around(value, index):
        field[centre] = value
        field[7:8] = west_ref[index : index + 1]
        field[143:144] = east_ref[index : index + 1]
        above = jnp.where(lane == 127, turn(north_all, 126 - 2 * index), turn(value, -1))
        below = jnp.where(lane == 0, turn(south_all, -2 * index), turn(value, 1))
        return field[low], field[high], above, below

    mask_around = around(mask, 16)
    weights = []
    for number in range(2):
        kappa = kappa_ref[number]
        near = around(kappa, 17 + number)
        four = [faces(mask, kappa, m, k) for m, k in zip(mask_around, near)]
        weights.append((1.0 - (four[0] + four[1] + four[2] + four[3]), *four))
    pressure_mask = PRESSURE * mask
    pressure_east, pressure_north = PRESSURE * mask_around[1], PRESSURE * mask_around[2]

    for level in range(4):
        density = None
        for name in range(4):
            own, *four = weights[name // 2]
            tilde = adjoint_ref[name, level] * mask
            near = around(tilde, 4 * name + level)
            total = own * tilde
            for weight, value in zip(four, near):
                total = total + weight * value
            if name == 0:
                density = pressure_east * tilde - pressure_mask * near[0]
            elif name == 1:
                density = density + pressure_north * tilde - pressure_mask * near[3]
            elif name == 2:
                total = total - ALPHA_T * density
            else:
                total = total + BETA_S * density
            out_ref[name, level] = total


def stencil(adjoint, land, diffusivity, west, east, south, north):
    return pl.pallas_call(
        stencil_kernel,
        out_shape=jax.ShapeDtypeStruct(adjoint.shape, F32),
        in_specs=[pl.BlockSpec(memory_space=pltpu.VMEM)] * 7,
        out_specs=pl.BlockSpec(memory_space=pltpu.VMEM),
        scratch_shapes=[pltpu.VMEM((152, 128), F32)],
        compiler_params=pltpu.CompilerParams(vmem_limit_bytes=24 * 2**20),
        name="stencil",
    )(adjoint, land, diffusivity, west, east, south, north)


def remove_kernel(pole_ref, chunks_ref, middle_ref, out_ref, high):
    south, north = pole_ref[0] != 0, pole_ref[1] != 0
    base = jnp.where(north, 64, 0)
    group = (8, 128)
    lane = lanes(group)
    polar = jnp.logical_or(south, north)
    for level in range(4):
        first = (pl.program_id(0) * 4 + level) * 4
        rows = chunks_ref[pl.ds(first, 4), 0:ROWS, :].astype(F32).reshape(64, 128)
        both = jnp.concatenate(
            [jnp.where(south, rows, 0.0), jnp.where(north, rows, 0.0)], axis=0
        )
        others = jnp.zeros(group, F32)
        for quarter in range(4):
            block = chunks_ref[first + quarter, ROWS:CHUNK, :].astype(F32)
            others = jnp.where(lane // 16 == quarter, turn(block, 16 * quarter), others)
        others = jnp.where(lane < 64, others, turn(others, 64))
        others = jnp.where(jnp.logical_and(lane // 64 == base // 64, polar), others, 0.0)
        high[1:129] = both.T
        high[0:1] = others[0:1]
        high[129:135] = others[1:7]
        out_ref[0, level] = middle_ref[0, level] - high[0:COLS]


def remove(pole, chunks, middle):
    return pl.pallas_call(
        remove_kernel,
        grid=(2,),
        out_shape=jax.ShapeDtypeStruct(middle.shape, F32),
        in_specs=[
            pl.BlockSpec(memory_space=pltpu.SMEM),
            pl.BlockSpec((RING, CHUNK, 128), lambda i: (0, 0, 0)),
            pl.BlockSpec((1, 4, COLS, 128), lambda i: (i, 0, 0, 0)),
        ],
        out_specs=pl.BlockSpec((1, 4, COLS, 128), lambda i: (i, 0, 0, 0)),
        scratch_shapes=[pltpu.VMEM((136, 128), F32)],
        input_output_aliases={2: 0},
        compiler_params=pltpu.CompilerParams(vmem_limit_bytes=24 * 2**20),
        name="remove",
    )(pole, chunks, middle)


def shift(value, axis, step, periodic):
    count = lax.axis_size(axis)
    pairs = [(i, (i + step) % count) for i in range(count) if periodic or 0 <= i + step < count]
    return lax.ppermute(value, axis, pairs)


def exchange(chunks):
    return lax.all_to_all(chunks, "lon", split_axis=0, concat_axis=0, tiled=True)


def local(adjoint, land, diffusivity, cutoff):
    lat_index = lax.axis_index("lat")
    northern = (lat_index == lax.axis_size("lat") - 1).astype(jnp.int32)
    southern = (lat_index == 0).astype(jnp.int32)
    quarter = lax.axis_index("lon") % 4
    cuts = lax.dynamic_slice_in_dim(cutoff, northern * PROWS + quarter * ROWS, ROWS, 0)
    square = jnp.broadcast_to(jnp.square(cuts.astype(F32))[:, None], (ROWS, 128))

    chunks = pack(northern[None], adjoint, land, diffusivity)
    circles = exchange(chunks)

    first, last, sides = edge(adjoint, land, diffusivity)
    west = shift(last, "lon", 1, True)
    east = shift(first, "lon", -1, True)
    south = shift(sides, "lat", 1, False)
    north = shift(sides, "lat", -1, False)
    middle = stencil(adjoint, land, diffusivity, west, east, south, north)

    removed = exchange(filter_rows(circles, square))
    return remove(jnp.stack([southern, northern]), removed, middle)


def solution(mesh):
    placed = (P(None, None, "lon", "lat"), P("lon", "lat"), P(None, "lon", "lat"), P())
    return jax.shard_map(
        local, mesh=mesh, in_specs=placed, out_specs=P(None, None, "lon", "lat"), check_vma=False
    )
```

```python
import math

import jax
import jax.numpy as jnp
import numpy as np
from jax import lax
from jax.experimental import pallas as pl
from jax.experimental.pallas import tpu as pltpu
from jax.sharding import PartitionSpec as P

PROWS = 64
PRESSURE = 0.3
ALPHA_T = 1.0
BETA_S = 0.8

RING = 32
COLS = 135
NLON = RING * COLS
INV = 23
CRT_RING = 3105
CRT_COLS = 1216
WAVES = 68
ROWS = 16
LEVELS = 4
FIELD = COLS * LEVELS
RIM = (0, FIELD - 4, 2 * FIELD - 8)
CHUNK = 24

MAIN = [lane + 1 for lane in range(128)]
EXTRA = [0] + list(range(129, 135))

F32 = jnp.float32
BF16 = jnp.bfloat16


def tables():
    order = np.array(MAIN + EXTRA + [0] * 121)
    used = np.array([1.0] * 135 + [0.0] * 121)
    waves = np.arange(WAVES)
    angle = 2.0 * math.pi * ((38 * order[:, None] * waves[None, :]) % COLS) / COLS
    forward = np.zeros((256, 256))
    forward[:, :WAVES] = np.cos(angle) * used[:, None]
    forward[:, 128 : 128 + WAVES] = -np.sin(angle) * used[:, None]
    weight = np.where(waves == 0, 1.0, 2.0) / NLON
    backward = forward.copy().T
    backward[:WAVES] *= NLON * weight[:, None]
    backward[128 : 128 + WAVES] *= NLON * weight[:, None]
    inverse_square = np.ones((RING, 128))
    for place in range(RING):
        kappa = int(format(place, "05b")[::-1], 2)
        ring_wave = 7 * kappa % RING
        k = (CRT_RING * ring_wave + CRT_COLS * waves) % NLON
        k = np.minimum(k, NLON - k)
        inverse_square[place, :WAVES] = np.where(k == 0, 1e6, 1.0 / np.maximum(k, 1) ** 2)
    return (
        jnp.asarray(forward, BF16),
        jnp.asarray(backward, BF16),
        jnp.asarray(inverse_square, F32),
    )


def turn(value, shift):
    size = value.shape[-1]
    shift %= size
    return value if shift == 0 else pltpu.roll(value, shift, value.ndim - 1)


def lanes(shape):
    return lax.broadcasted_iota(jnp.int32, shape, len(shape) - 1)


def sublanes(shape):
    return lax.broadcasted_iota(jnp.int32, shape, len(shape) - 2)


def level_rows(field, level):
    return pl.ds(FIELD * field + level, COLS, stride=LEVELS)


def faces(mask, kappa, mask_near, kappa_near):
    return 0.5 * (kappa + kappa_near) * mask * mask_near


def poles():
    index = lax.axis_index("lat")
    return index == 0, index == lax.axis_size("lat") - 1


def at_pole():
    south, north = poles()
    return jnp.logical_or(south, north)


def even(axis):
    return lax.axis_index(axis) % 2 == 0


def pack_kernel(*refs):
    @pl.when(at_pole())
    def _():
        pack_rows(*refs)


def pack_rows(adjoint_ref, land_ref, kappa_ref, out_ref, field, part):
    north = poles()[1]
    whole = (COLS, 128)
    low, high = pl.ds(7, COLS), pl.ds(9, COLS)
    centre = pl.ds(8, COLS)
    zero = jnp.zeros((8, 128), F32)
    field[0:8] = zero
    field[136:144] = zero
    field[144:152] = zero
    lane = lanes(whole)
    mask = land_ref[...].astype(F32)
    kappa = kappa_ref[:, 0, :]

    field[centre] = kappa
    kappa_west, kappa_east = field[low], field[high]
    field[centre] = mask
    mask_west, mask_east = field[low], field[high]
    west = faces(mask, kappa, mask_west, kappa_west)
    east = faces(mask, kappa, mask_east, kappa_east)
    up = faces(mask, kappa, jnp.where(lane == 127, 0.0, turn(mask, -1)), turn(kappa, -1))
    down = faces(mask, kappa, jnp.where(lane == 0, 0.0, turn(mask, 1)), turn(kappa, 1))
    own = 1.0 - (west + east + up + down)

    group = (8, 128)
    slot = sublanes(group)
    lane8 = lanes(group)
    edge_fixed = jnp.zeros(group, F32)
    for place, row in ((1, kappa[134:135]), (2, mask[134:135]), (4, kappa[0:1]), (5, mask[0:1])):
        edge_fixed = jnp.where(slot == place, row, edge_fixed)
    part[136:144] = zero
    for index in range(8):
        tilde = adjoint_ref[level_rows(index // 4, index % 4)] * mask
        field[centre] = tilde
        partial = (
            own * tilde
            + west * field[low]
            + east * field[high]
            + up * turn(tilde, -1)
            + down * turn(tilde, 1)
        )
        part[0:COLS] = partial
        turned = part[pl.ds(1, 128)].T
        chosen = jnp.where(north, turned[64:128], turned[0:64])
        others = jnp.where(slot == 0, partial[0:1], part[128:136])
        others = jnp.where(slot == 7, 0.0, others)
        edges = jnp.where(slot == 0, tilde[134:135], jnp.where(slot == 3, tilde[0:1], edge_fixed))
        others = jnp.where(north, turn(others, 64), others)
        edges = jnp.where(north, turn(edges, 64), edges)
        for quarter in range(4):
            place = 4 * index + quarter
            out_ref[place, 0:ROWS] = chosen[16 * quarter : 16 * quarter + 16].astype(BF16)
            out_ref[place, ROWS:CHUNK] = jnp.where(
                lane8 < 16, turn(others, -16 * quarter), turn(edges, 16 - 16 * quarter)
            ).astype(BF16)


def pack(adjoint, land, diffusivity):
    return pl.pallas_call(
        pack_kernel,
        grid=(1,),
        out_shape=jax.ShapeDtypeStruct((RING, CHUNK, 128), BF16),
        in_specs=[
            pl.BlockSpec((2 * FIELD, 128), lambda i: (0, 0)),
            pl.BlockSpec((COLS, 128), lambda i: (0, 0)),
            pl.BlockSpec((COLS, 2, 128), lambda i: (0, 0, 0)),
        ],
        out_specs=pl.BlockSpec((RING, CHUNK, 128), lambda i: (0, 0, 0)),
        scratch_shapes=[pltpu.VMEM((152, 128), F32), pltpu.VMEM((144, 128), F32)],
        compiler_params=pltpu.CompilerParams(vmem_limit_bytes=60 * 2**20),
        name="pack",
    )(adjoint, land, diffusivity)


def times(re, im, angle_index, count, sign):
    eighth = 8 * angle_index // count if 8 * angle_index % count == 0 else None
    half = math.sqrt(0.5)
    if eighth == 0:
        return re, im
    if eighth == 2:
        return (-im, re) if sign > 0 else (im, -re)
    if eighth == 1:
        if sign > 0:
            return half * (re - im), half * (re + im)
        return half * (re + im), half * (im - re)
    if eighth == 3:
        if sign > 0:
            return -half * (re + im), half * (re - im)
        return half * (im - re), -half * (re + im)
    cos = math.cos(2.0 * math.pi * angle_index / count)
    sin = sign * math.sin(2.0 * math.pi * angle_index / count)
    return cos * re - sin * im, sin * re + cos * im


def fourier(values):
    half = RING // 2
    while half:
        for start in range(0, RING, 2 * half):
            for i in range(half):
                a, b = start + i, start + i + half
                (ar, ai), (br, bi) = values[a], values[b]
                values[a] = (ar + br, ai + bi)
                values[b] = times(ar - br, ai - bi, i, 2 * half, -1)
        half //= 2


def fourier_back(values):
    half = 1
    while half < RING:
        for start in range(0, RING, 2 * half):
            for i in range(half):
                a, b = start + i, start + i + half
                ar, ai = values[a]
                br, bi = times(*values[b], i, 2 * half, 1)
                values[a] = (ar + br, ai + bi)
                values[b] = (ar - br, ai - bi)
        half *= 2


def slot_shift(value, sign):
    slot = lanes(value.shape) % 8
    for bit in range(5):
        moved = turn(value, sign * 8 * 2**bit)
        picked = jnp.zeros(value.shape, jnp.bool_)
        for place, column in enumerate(EXTRA):
            if (INV * column % RING) >> bit & 1:
                picked = jnp.logical_or(picked, slot == place)
        value = jnp.where(picked, moved, value)
    return value


def filter_kernel(*refs):
    @pl.when(at_pole())
    def _():
        filter_circles(*refs)


def filter_circles(in_ref, square_ref, forward_ref, backward_ref, inverse_ref, out_ref, held, wave):
    tile = (ROWS, 128)
    spare = in_ref[:, ROWS:CHUNK, :].astype(F32).reshape(256, 128)
    spare = jnp.concatenate([spare[0:128].T[0:32], spare[128:256].T[0:32]], axis=1)
    others, edges = spare[0:16], spare[16:32]
    slot = lanes(others.shape) % 8
    beyond = turn(edges, -11)
    flux = (beyond - edges) * turn(0.5 * (beyond + edges), -1) * turn(beyond * edges, -2)
    others = others + jnp.where(slot == 6, turn(flux, 6), 0.0)
    others = others - jnp.where(slot == 0, turn(flux, 8), 0.0)
    others = slot_shift(others, 1)

    column = lanes(tile) + 1
    rows = [in_ref[INV * t % RING, 0:ROWS, :] for t in range(RING)]
    for bit in range(5):
        picked = (column >> bit) & 1 == 1
        rows = [jnp.where(picked, rows[(t - 2**bit) % RING], rows[t]) for t in range(RING)]
    for t in range(RING):
        place = INV * t % RING
        held[pl.ds(ROWS * t, ROWS), 0:128] = rows[t]
        side = others[:, 128 * (place // 16) : 128 * (place // 16) + 128]
        held[pl.ds(ROWS * t, ROWS), 128:256] = turn(side, -8 * (place % 16)).astype(BF16)

    wave[...] = jnp.dot(held[...], forward_ref[...], preferred_element_type=F32)
    for half in range(2):
        rows_of = [pl.ds(ROWS * t + 8 * half, 8) for t in range(RING)]
        values = [(wave[r, 0:128], wave[r, 128:256]) for r in rows_of]
        fourier(values)
        square = square_ref[8 * half : 8 * half + 8]
        for t in range(RING):
            keep = jnp.maximum(0.0, 1.0 - square * inverse_ref[t : t + 1]) * (1.0 / NLON)
            values[t] = (values[t][0] * keep, values[t][1] * keep)
        fourier_back(values)
        for t in range(RING):
            wave[rows_of[t], 0:128] = values[t][0]
            wave[rows_of[t], 128:256] = values[t][1]
    wave[...] = jnp.dot(wave[...].astype(BF16), backward_ref[...], preferred_element_type=F32)

    rows = [wave[pl.ds(ROWS * t, ROWS), 0:128] for t in range(RING)]
    for bit in range(5):
        picked = (column >> bit) & 1 == 1
        rows = [jnp.where(picked, rows[(t + 2**bit) % RING], rows[t]) for t in range(RING)]
    for d in range(RING):
        out_ref[d, 0:ROWS] = rows[7 * d % RING].astype(BF16)
    sides = [jnp.zeros(tile, F32), jnp.zeros(tile, F32)]
    for t in range(RING):
        place = INV * t % RING
        sides[place // 16] += turn(wave[pl.ds(ROWS * t, ROWS), 128:256], 8 * (place % 16))
    others = slot_shift(jnp.concatenate(sides, axis=1), -1)
    blank = jnp.zeros((112, 128), F32)
    for half in range(2):
        back = jnp.concatenate([others[:, 128 * half : 128 * half + 128], blank], axis=0).T
        out_ref[16 * half : 16 * half + 16, ROWS:CHUNK] = back.reshape(16, 8, 128).astype(BF16)


def filter_rows(chunks, square):
    forward, backward, inverse_square = tables()
    return pl.pallas_call(
        filter_kernel,
        out_shape=jax.ShapeDtypeStruct((RING, CHUNK, 128), BF16),
        in_specs=[pl.BlockSpec(memory_space=pltpu.VMEM)] * 5,
        out_specs=pl.BlockSpec(memory_space=pltpu.VMEM),
        scratch_shapes=[
            pltpu.VMEM((RING * ROWS, 256), BF16),
            pltpu.VMEM((RING * ROWS, 256), F32),
        ],
        compiler_params=pltpu.CompilerParams(vmem_limit_bytes=24 * 2**20),
        name="filter",
    )(chunks, square, forward, backward, inverse_square)


def edge_kernel(adjoint_ref, land_ref, kappa_ref, near_ref, far_ref, side_ref):
    lon_even = even("lon")
    whole = (COLS, 128)
    lane = lanes(whole)
    mask = land_ref[...].astype(F32)
    sides = jnp.zeros(whole, F32)
    near_ref[...] = jnp.zeros((24, 128), F32)
    far_ref[...] = jnp.zeros((24, 128), F32)
    for index in range(19):
        if index < 16:
            value = adjoint_ref[level_rows(index // 4, index % 4)] * mask
        elif index == 16:
            value = mask
        else:
            value = kappa_ref[:, index - 17, :]
        near_ref[index : index + 1] = jnp.where(lon_even, value[134:135], value[0:1])
        far_ref[index : index + 1] = jnp.where(lon_even, value[0:1], value[134:135])
        sides = jnp.where(lane // 2 == index, turn(value, 2 * index + 1), sides)
    side_ref[...] = sides


def edge(adjoint, land, diffusivity):
    return pl.pallas_call(
        edge_kernel,
        out_shape=(
            jax.ShapeDtypeStruct((24, 128), F32),
            jax.ShapeDtypeStruct((24, 128), F32),
            jax.ShapeDtypeStruct((COLS, 128), F32),
        ),
        in_specs=[pl.BlockSpec(memory_space=pltpu.VMEM)] * 3,
        out_specs=[pl.BlockSpec(memory_space=pltpu.VMEM)] * 3,
        compiler_params=pltpu.CompilerParams(vmem_limit_bytes=24 * 2**20),
        name="edge",
    )(adjoint, land, diffusivity)


def stencil_kernel(
    adjoint_ref,
    land_ref,
    kappa_ref,
    near_side_ref,
    far_side_ref,
    out_ref,
    flow_ref,
    rim_ref,
    field,
):
    whole = (COLS, 128)
    lane = lanes(whole)
    centre, low, high = pl.ds(8, COLS), pl.ds(7, COLS), pl.ds(9, COLS)
    lat_even = even("lat")
    south_all = jnp.where(lat_even, far_side_ref[...], near_side_ref[...])
    north_all = jnp.where(lat_even, near_side_ref[...], far_side_ref[...])
    mask = land_ref[...].astype(F32)
    field[0:8] = jnp.zeros((8, 128), F32)
    field[136:144] = jnp.zeros((8, 128), F32)
    field[144:152] = jnp.zeros((8, 128), F32)

    def around(value, index):
        field[centre] = value
        above = jnp.where(lane == 127, turn(north_all, 126 - 2 * index), turn(value, -1))
        below = jnp.where(lane == 0, turn(south_all, -2 * index), turn(value, 1))
        return field[low], field[high], above, below

    mask_around = around(mask, 16)
    weights = []
    for number in range(2):
        kappa = kappa_ref[:, number, :]
        near = around(kappa, 17 + number)
        four = [faces(mask, kappa, m, k) for m, k in zip(mask_around, near)]
        weights.append((1.0 - (four[0] + four[1] + four[2] + four[3]), *four))
    pressure_mask = PRESSURE * mask
    pressure_east, pressure_north = PRESSURE * mask_around[1], PRESSURE * mask_around[2]

    for level in range(4):
        density = None
        for name in range(4):
            own, *four = weights[name // 2]
            tilde = adjoint_ref[level_rows(name, level)] * mask
            near = around(tilde, 4 * name + level)
            total = own * tilde
            for weight, value in zip(four, near):
                total = total + weight * value
            if name == 0:
                density = pressure_east * tilde - pressure_mask * near[0]
            elif name == 1:
                density = density + pressure_north * tilde - pressure_mask * near[3]
            elif name == 2:
                total = total - ALPHA_T * density
            else:
                total = total + BETA_S * density
            if name < 2:
                flow_ref[level_rows(name, level)] = total
            else:
                out_ref[level_rows(name - 2, level)] = total
    for number, start in enumerate(RIM):
        rim_ref[8 * number : 8 * number + 8] = out_ref[start : start + 8]


def stencil(adjoint, land, diffusivity, near_side, far_side):
    return pl.pallas_call(
        stencil_kernel,
        grid=(1,),
        out_shape=(
            jax.ShapeDtypeStruct(adjoint.shape, F32),
            jax.ShapeDtypeStruct((2 * FIELD, 128), F32),
            jax.ShapeDtypeStruct((24, 128), F32),
        ),
        in_specs=[pl.BlockSpec(memory_space=pltpu.VMEM)] * 5,
        out_specs=[
            pl.BlockSpec((2 * FIELD, 128), lambda i: (1, 0)),
            pl.BlockSpec(memory_space=pltpu.VMEM),
            pl.BlockSpec(memory_space=pltpu.VMEM),
        ],
        scratch_shapes=[pltpu.VMEM((152, 128), F32)],
        compiler_params=pltpu.CompilerParams(vmem_limit_bytes=24 * 2**20),
        name="stencil",
    )(adjoint, land, diffusivity, near_side, far_side)


def crossing(own_near, own_far, near, far):
    lon_even = even("lon")
    own_west, own_east = jnp.where(lon_even, own_far, own_near), jnp.where(lon_even, own_near, own_far)
    west, east = jnp.where(lon_even, far, near), jnp.where(lon_even, near, far)

    def flux(own, other):
        masks = own[16:17] * other[16:17]
        first, second = (0.5 * (own[k : k + 1] + other[k : k + 1]) * masks for k in (17, 18))
        step = other[0:16] - own[0:16]
        return first * step[0:8], second * step[8:16]

    west_flow, west_tracer = flux(own_west, west)
    east_flow, east_tracer = flux(own_east, east)
    west_density = -PRESSURE * own_west[16:17] * west[0:4]
    east_density = PRESSURE * east[16:17] * own_east[0:4]
    west_tracer += jnp.concatenate([-ALPHA_T * west_density, BETA_S * west_density], axis=0)
    east_tracer += jnp.concatenate([-ALPHA_T * east_density, BETA_S * east_density], axis=0)
    return west_flow, east_flow, west_tracer, east_tracer


def remove_kernel(
    chunks_ref,
    flow_ref,
    rim_ref,
    own_near_ref,
    own_far_ref,
    near_ref,
    far_ref,
    whole_ref,
    out_ref,
    new_flow,
    new_rim,
    high,
    done,
):
    del whole_ref
    west, east, west_tracer, east_tracer = crossing(
        own_near_ref[...], own_far_ref[...], near_ref[...], far_ref[...]
    )
    none = jnp.zeros((4, 128), F32)
    new_rim[...] = rim_ref[...] + jnp.concatenate(
        [west_tracer[0:4], none, east_tracer[0:4], west_tracer[4:8], none, east_tracer[4:8]], axis=0
    )
    copies = [
        pltpu.make_async_copy(
            new_rim.at[pl.ds(8 * number, 8)],
            out_ref.at[pl.ds(2 * FIELD + start, 8)],
            done.at[number],
        )
        for number, start in enumerate(RIM)
    ]
    polar = at_pole()
    for copy in copies:
        copy.start()
    for name, (start, size) in enumerate(((0, FIELD - 4), (FIELD - 4, FIELD + 4))):

        @pl.when(polar)
        def _():
            remove_waves(name, chunks_ref, flow_ref, new_flow, high)

        rows = pl.ds(FIELD * name, FIELD)

        @pl.when(jnp.logical_not(polar))
        def _():
            new_flow[rows] = flow_ref[rows]

        first, last = pl.ds(FIELD * name, 4), pl.ds(FIELD * name + FIELD - 4, 4)
        new_flow[first] = new_flow[first] + west[4 * name : 4 * name + 4]
        new_flow[last] = new_flow[last] + east[4 * name : 4 * name + 4]
        rows = pl.ds(start, size)
        copy = pltpu.make_async_copy(new_flow.at[rows], out_ref.at[rows], done.at[3 + name])
        copy.start()
        copies.append(copy)
    for copy in copies:
        copy.wait()


def remove_waves(name, chunks_ref, flow_ref, out_ref, high):
    south, north = poles()
    group = (8, 128)
    lane = lanes(group)
    for level in range(4):
        first = 16 * name + 4 * level
        rows = chunks_ref[first : first + 4, 0:ROWS, :].astype(F32).reshape(64, 128)
        both = jnp.concatenate([jnp.where(south, rows, 0.0), jnp.where(north, rows, 0.0)], axis=0)
        others = jnp.zeros(group, F32)
        for quarter in range(4):
            block = chunks_ref[first + quarter, ROWS:CHUNK, :].astype(F32)
            others = jnp.where(lane // 16 == quarter, turn(block, 16 * quarter), others)
        others = jnp.where(north, turn(others, 64), others)
        high[1:129] = both.T
        high[0:1] = others[0:1]
        high[129:135] = others[1:7]
        rows_of = level_rows(name, level)
        out_ref[rows_of] = flow_ref[rows_of] - high[0:COLS]


def remove(chunks, flow, rim, own_near, own_far, near, far, whole):
    return pl.pallas_call(
        remove_kernel,
        out_shape=jax.ShapeDtypeStruct(whole.shape, F32),
        in_specs=[pl.BlockSpec(memory_space=pltpu.VMEM)] * 7 + [pl.BlockSpec(memory_space=pl.ANY)],
        out_specs=pl.BlockSpec(memory_space=pl.ANY),
        scratch_shapes=[
            pltpu.VMEM((2 * FIELD, 128), F32),
            pltpu.VMEM((24, 128), F32),
            pltpu.VMEM((136, 128), F32),
            pltpu.SemaphoreType.DMA((5,)),
        ],
        input_output_aliases={7: 0},
        compiler_params=pltpu.CompilerParams(vmem_limit_bytes=24 * 2**20),
        name="remove",
    )(chunks, flow, rim, own_near, own_far, near, far, whole)


def swap(value, axis, first):
    count = lax.axis_size(axis)
    pairs = []
    for a in range(first, count, 2):
        b = a + 1
        if b == count:
            if axis == "lat":
                continue
            b = 0
        pairs += [(a, b), (b, a)]
    return lax.ppermute(value, axis, pairs)


def exchange(chunks):
    return lax.all_to_all(chunks, "lon", split_axis=0, concat_axis=0, tiled=True)


def local(adjoint, land, diffusivity, cutoff):
    lon_index, lat_index = lax.axis_index("lon"), lax.axis_index("lat")
    first_cut = jnp.where(lat_index == lax.axis_size("lat") - 1, PROWS, 0) + lon_index % 4 * ROWS
    cuts = lax.dynamic_slice_in_dim(cutoff, first_cut, ROWS, 0)
    square = jnp.broadcast_to(jnp.square(cuts.astype(F32))[:, None], (ROWS, 128))

    shape = adjoint.shape
    fields = jnp.transpose(adjoint, (0, 2, 1, 3)).reshape(-1, shape[3])
    kappas = jnp.transpose(diffusivity, (1, 0, 2))

    chunks = pack(fields, land, kappas)
    circles = exchange(chunks)
    own_near, own_far, sides = edge(fields, land, kappas)
    near_side = swap(sides, "lat", 0)
    far_side = swap(sides, "lat", 1)
    circles, near_side, far_side = lax.optimization_barrier((circles, near_side, far_side))

    filtered = filter_rows(circles, square)
    filtered, own_near, own_far = lax.optimization_barrier((filtered, own_near, own_far))
    removed = exchange(filtered)
    near = swap(own_near, "lon", 0)
    far = swap(own_far, "lon", 1)
    whole, flow, rim = stencil(fields, land, kappas, near_side, far_side)

    out = remove(removed, flow, rim, own_near, own_far, near, far, whole)
    return jnp.transpose(out.reshape(shape[0], shape[2], shape[1], shape[3]), (0, 2, 1, 3))


def solution(mesh):
    placed = (P(None, None, "lon", "lat"), P("lon", "lat"), P(None, "lon", "lat"), P())
    return jax.shard_map(
        local, mesh=mesh, in_specs=placed, out_specs=P(None, None, "lon", "lat"), check_vma=False
    )
```

```python
import math

import jax
import jax.numpy as jnp
import numpy as np
from jax import lax
from jax.experimental import pallas as pl
from jax.experimental.pallas import tpu as pltpu
from jax.sharding import PartitionSpec as P

PROWS = 64
PRESSURE = 0.3
ALPHA_T = 1.0
BETA_S = 0.8

RING = 32
COLS = 135
NLON = RING * COLS
INV = 23
CRT_RING = 3105
CRT_COLS = 1216
WAVES = 68
ROWS = 16
LEVELS = 4
FIELD = COLS * LEVELS
RIM = (0, FIELD - 4, 2 * FIELD - 8)
CHUNK = ROWS + 2
THIRD = 48
PART = 8 * CHUNK

MAIN = [lane + 1 for lane in range(128)]
EXTRA = [0] + list(range(129, 135)) + [None]

F32 = jnp.float32
BF16 = jnp.bfloat16


def tables():
    waves = np.arange(WAVES)

    def transform(slots):
        columns = MAIN + [column for column in slots for _ in range(ROWS)]
        used = np.array([[float(column is not None)] for column in columns])
        order = np.array([[column or 0] for column in columns])
        angle = 2.0 * math.pi * ((38 * order * waves) % COLS) / COLS
        table = np.zeros((256, 256))
        table[:, :WAVES] = np.cos(angle) * used
        table[:, 128 : 128 + WAVES] = -np.sin(angle) * used
        return table

    forward, backward = transform(EXTRA), transform(EXTRA[::-1]).T
    backward *= np.where(np.arange(256) % 128 == 0, 1.0, 2.0)[:, None]
    inverse_square = np.ones((RING, 128))
    for place in range(RING):
        kappa = int(format(place, "05b")[::-1], 2)
        ring_wave = 7 * kappa % RING
        k = (CRT_RING * ring_wave + CRT_COLS * waves) % NLON
        k = np.minimum(k, NLON - k)
        inverse_square[place, :WAVES] = np.where(k == 0, 1e6, 1.0 / np.maximum(k, 1) ** 2)
    return (
        jnp.asarray(forward, BF16),
        jnp.asarray(backward, BF16),
        jnp.asarray(inverse_square, F32),
    )


def turn(value, shift):
    size = value.shape[-1]
    shift %= size
    return value if shift == 0 else pltpu.roll(value, shift, value.ndim - 1)


def lanes(shape):
    return lax.broadcasted_iota(jnp.int32, shape, len(shape) - 1)


def sublanes(shape):
    return lax.broadcasted_iota(jnp.int32, shape, len(shape) - 2)


def level_rows(field, level):
    return pl.ds(FIELD * field + level, COLS, stride=LEVELS)


def faces(mask, kappa, mask_near, kappa_near):
    return 0.5 * (kappa + kappa_near) * mask * mask_near


def poles():
    index = lax.axis_index("lat")
    return index == 0, index == lax.axis_size("lat") - 1


def at_pole():
    south, north = poles()
    return jnp.logical_or(south, north)


def even(axis):
    return lax.axis_index(axis) % 2 == 0


def spread(value):
    return pltpu.roll(value, 0, 1, stride=ROWS, stride_axis=0)


def pack_kernel(*refs):
    @pl.when(at_pole())
    def _():
        pack_rows(*refs)


def pack_rows(
    adjoint_hbm, land_hbm, kappa_hbm, out_hbm, rows, land, kappas, field, part, chunks, arrived, left
):
    def arrival(source, target, number):
        copy = pltpu.make_async_copy(source, target, arrived.at[number])
        copy.start()
        return copy

    first = arrival(land_hbm, land, 0), arrival(kappa_hbm, kappas, 1)
    half = FIELD + 4
    fields = [
        arrival(adjoint_hbm.at[pl.ds(start, size)], rows.at[pl.ds(start, size)], number)
        for number, start, size in ((2, 0, half), (3, half, 2 * FIELD - half))
    ]
    north = poles()[1]
    whole = (COLS, 128)
    low, high = pl.ds(7, COLS), pl.ds(9, COLS)
    centre = pl.ds(8, COLS)
    zero = jnp.zeros((8, 128), F32)
    field[0:8] = zero
    field[136:144] = zero
    field[144:152] = zero
    lane = lanes(whole)
    chosen = (lanes((PROWS, 128)) == sublanes((PROWS, 128)) + jnp.where(north, 64, 0)).astype(BF16)
    group = (8, 128)
    slot = sublanes(group)
    in_slot = lanes(group) // ROWS == slot

    for copy in first:
        copy.wait()
    mask = land[...].astype(F32)
    kappa = kappas[:, 0, :]
    field[centre] = kappa
    kappa_west, kappa_east = field[low], field[high]
    field[centre] = mask
    mask_west, mask_east = field[low], field[high]
    west = faces(mask, kappa, mask_west, kappa_west)
    east = faces(mask, kappa, mask_east, kappa_east)
    up = faces(mask, kappa, jnp.where(lane == 127, 0.0, turn(mask, -1)), turn(kappa, -1))
    down = faces(mask, kappa, jnp.where(lane == 0, 0.0, turn(mask, 1)), turn(kappa, 1))
    own = 1.0 - (west + east + up + down)
    edge_fixed = jnp.zeros(group, F32)
    for place, row in ((1, kappa[134:135]), (2, mask[134:135]), (4, kappa[0:1]), (5, mask[0:1])):
        edge_fixed = jnp.where(slot == place, row, edge_fixed)

    copies = []
    for name in range(2):
        fields[name].wait()
        for level in range(4):
            tilde = rows[level_rows(name, level)] * mask
            field[centre] = tilde
            partial = (
                own * tilde
                + west * field[low]
                + east * field[high]
                + up * turn(tilde, -1)
                + down * turn(tilde, 1)
            )
            part[pl.ds(7, COLS)] = partial
            turned = lax.dot_general(
                chosen,
                part[8:136].astype(BF16),
                (((1,), (1,)), ((), ())),
                preferred_element_type=F32,
            ).astype(BF16)
            others = jnp.where(slot == 0, partial[0:1], part[pl.ds(135, 8)])
            others = jnp.where(slot == 7, 0.0, others)
            edges = jnp.where(slot == 0, tilde[134:135], jnp.where(slot == 3, tilde[0:1], edge_fixed))
            others = spread(jnp.where(north, turn(others, 64), others))
            edges = spread(jnp.where(north, turn(edges, 64), edges))
            for quarter in range(4):
                place = CHUNK * (16 * name + 4 * level + quarter)
                chunks[place : place + ROWS] = turned[ROWS * quarter : ROWS * quarter + ROWS]
                two = [
                    jnp.sum(
                        jnp.where(in_slot, turn(value, -ROWS * quarter), 0.0), axis=0, keepdims=True
                    )
                    for value in (others, edges)
                ]
                chunks[place + ROWS : place + CHUNK] = jnp.concatenate(two, axis=0).astype(BF16)
            if level % 2:
                number = 2 * name + level // 2
                span = pl.ds(PART * number, PART)
                copy = pltpu.make_async_copy(chunks.at[span], out_hbm.at[span], left.at[number])
                copy.start()
                copies.append(copy)
    for copy in copies:
        copy.wait()


def pack(adjoint, land, diffusivity):
    return pl.pallas_call(
        pack_kernel,
        out_shape=jax.ShapeDtypeStruct((RING * CHUNK, 128), BF16),
        in_specs=[pl.BlockSpec(memory_space=pl.ANY)] * 3,
        out_specs=pl.BlockSpec(memory_space=pl.ANY),
        scratch_shapes=[
            pltpu.VMEM((2 * FIELD, 128), F32),
            pltpu.VMEM((COLS, 128), jnp.int32),
            pltpu.VMEM((COLS, 2, 128), F32),
            pltpu.VMEM((152, 128), F32),
            pltpu.VMEM((144, 128), F32),
            pltpu.VMEM((RING * CHUNK, 128), BF16),
            pltpu.SemaphoreType.DMA((4,)),
            pltpu.SemaphoreType.DMA((4,)),
        ],
        compiler_params=pltpu.CompilerParams(vmem_limit_bytes=60 * 2**20),
        name="pack",
    )(adjoint, land, diffusivity)


def times(re, im, angle_index, count, sign):
    eighth = 8 * angle_index // count if 8 * angle_index % count == 0 else None
    half = math.sqrt(0.5)
    if eighth == 0:
        return re, im
    if eighth == 2:
        return (-im, re) if sign > 0 else (im, -re)
    if eighth == 1:
        if sign > 0:
            return half * (re - im), half * (re + im)
        return half * (re + im), half * (im - re)
    if eighth == 3:
        if sign > 0:
            return -half * (re + im), half * (re - im)
        return half * (im - re), -half * (re + im)
    cos = math.cos(2.0 * math.pi * angle_index / count)
    sin = sign * math.sin(2.0 * math.pi * angle_index / count)
    return cos * re - sin * im, sin * re + cos * im


def fourier(values):
    half = RING // 2
    while half:
        for start in range(0, RING, 2 * half):
            for i in range(half):
                a, b = start + i, start + i + half
                (ar, ai), (br, bi) = values[a], values[b]
                values[a] = (ar + br, ai + bi)
                values[b] = times(ar - br, ai - bi, i, 2 * half, -1)
        half //= 2


def fourier_back(values):
    half = 1
    while half < RING:
        for start in range(0, RING, 2 * half):
            for i in range(half):
                a, b = start + i, start + i + half
                ar, ai = values[a]
                br, bi = times(*values[b], i, 2 * half, 1)
                values[a] = (ar + br, ai + bi)
                values[b] = (ar - br, ai - bi)
        half *= 2


def ring_shift(value, step, columns):
    slot = lanes(value.shape) // ROWS
    for bit in range(5):
        moved = pltpu.roll(value, step * 2**bit % RING, 0)
        picked = jnp.zeros(value.shape, jnp.bool_)
        for place, column in enumerate(columns):
            if (column or 0) >> bit & 1:
                picked = jnp.logical_or(picked, slot == place)
        value = jnp.where(picked, moved, value)
    return value


def filter_kernel(*refs):
    @pl.when(at_pole())
    def _():
        filter_circles(*refs)


def filter_circles(
    in_ref, square_ref, forward_ref, backward_ref, inverse_ref, out_hbm, held, wave, pair, chunks, left
):
    tile = (ROWS, 128)
    own_row = lanes(tile) % ROWS == sublanes(tile)
    column = lanes(tile) + 1
    rows = []
    for t in range(RING):
        start = CHUNK * (INV * t % RING)
        rows.append(in_ref[start : start + ROWS])
        pair[2 * t : 2 * t + 2] = in_ref[start + ROWS : start + CHUNK].astype(F32)
    for bit in range(5):
        picked = (column >> bit) & 1 == 1
        rows = [jnp.where(picked, rows[(t - 2**bit) % RING], rows[t]) for t in range(RING)]
    for t in range(RING):
        held[ROWS * t : ROWS * t + ROWS, 0:128] = rows[t]

    others, edges = pair[pl.ds(0, RING, stride=2)], pair[pl.ds(1, RING, stride=2)]
    slot = lanes(others.shape) // ROWS
    beyond = turn(pltpu.roll(edges, RING - 7, 0), -3 * ROWS)
    flux = (beyond - edges) * turn(0.5 * (beyond + edges), -ROWS) * turn(beyond * edges, -2 * ROWS)
    others = others + jnp.where(slot == 6, turn(flux, 6 * ROWS), 0.0)
    others = others - jnp.where(slot == 0, pltpu.roll(flux, 7, 0), 0.0)
    pair[0:RING] = ring_shift(others, 1, EXTRA)
    for t in range(RING):
        side = jnp.where(own_row, pair[t : t + 1], 0.0)
        held[ROWS * t : ROWS * t + ROWS, 128:256] = side.astype(BF16)

    wave[...] = jnp.dot(held[...], forward_ref[...], preferred_element_type=F32)
    for half in range(2):
        rows_of = [pl.ds(ROWS * t + 8 * half, 8) for t in range(RING)]
        values = [(wave[r, 0:128], wave[r, 128:256]) for r in rows_of]
        fourier(values)
        square = square_ref[8 * half : 8 * half + 8]
        for t in range(RING):
            keep = jnp.maximum(0.0, 1.0 - square * inverse_ref[t : t + 1]) * (1.0 / NLON)
            values[t] = (values[t][0] * keep, values[t][1] * keep)
        fourier_back(values)
        for t in range(RING):
            wave[rows_of[t], 0:128] = values[t][0]
            wave[rows_of[t], 128:256] = values[t][1]
    wave[...] = jnp.dot(wave[...].astype(BF16), backward_ref[...], preferred_element_type=F32)

    for t in range(RING):
        side = jnp.where(own_row, wave[ROWS * t : ROWS * t + ROWS, 128:256], 0.0)
        held[ROWS * t : ROWS * t + ROWS, 128:256] = side.astype(BF16)
    shape = (RING, RING * ROWS)
    gather = (lanes(shape) // ROWS == sublanes(shape)).astype(BF16)
    others = jnp.dot(gather, held[:, 128:256], preferred_element_type=F32)
    pair[0:RING] = ring_shift(others, -1, EXTRA[::-1])

    rows = [wave[ROWS * t : ROWS * t + ROWS, 0:128].astype(BF16) for t in range(RING)]
    for bit in range(5):
        picked = (column >> bit) & 1 == 1
        rows = [jnp.where(picked, rows[(t + 2**bit) % RING], rows[t]) for t in range(RING)]
    copies = []
    for d in range(RING):
        place = 7 * d % RING
        chunks[CHUNK * d : CHUNK * d + ROWS] = rows[place]
        last = jnp.broadcast_to(pair[place : place + 1], (2, 128))
        chunks[CHUNK * d + ROWS : CHUNK * d + CHUNK] = last.astype(BF16)
        if d % 8 == 7:
            span = pl.ds(PART * (d // 8), PART)
            copy = pltpu.make_async_copy(chunks.at[span], out_hbm.at[span], left.at[d // 8])
            copy.start()
            copies.append(copy)
    for copy in copies:
        copy.wait()


def filter_rows(chunks, square):
    forward, backward, inverse_square = tables()
    return pl.pallas_call(
        filter_kernel,
        out_shape=jax.ShapeDtypeStruct((RING * CHUNK, 128), BF16),
        in_specs=[pl.BlockSpec(memory_space=pltpu.VMEM)] * 5,
        out_specs=pl.BlockSpec(memory_space=pl.ANY),
        scratch_shapes=[
            pltpu.VMEM((RING * ROWS, 256), BF16),
            pltpu.VMEM((RING * ROWS, 256), F32),
            pltpu.VMEM((2 * RING, 128), F32),
            pltpu.VMEM((RING * CHUNK, 128), BF16),
            pltpu.SemaphoreType.DMA((4,)),
        ],
        compiler_params=pltpu.CompilerParams(vmem_limit_bytes=24 * 2**20),
        name="filter",
    )(chunks, square, forward, backward, inverse_square)


def edge_kernel(adjoint_ref, land_ref, kappa_ref, near_ref, far_ref, side_ref, unfolded):
    lon_even = even("lon")
    whole = (COLS, 128)
    lane = lanes(whole)
    mask = land_ref[...].astype(F32)
    sides = jnp.zeros(whole, F32)
    near_ref[...] = jnp.zeros((24, 128), F32)
    far_ref[...] = jnp.zeros((24, 128), F32)
    for index in range(19):
        if index < 16:
            value = adjoint_ref[level_rows(index // 4, index % 4)] * mask
        elif index == 16:
            value = mask
        else:
            value = kappa_ref[:, index - 17, :]
        near_ref[index : index + 1] = jnp.where(lon_even, value[134:135], value[0:1])
        far_ref[index : index + 1] = jnp.where(lon_even, value[0:1], value[134:135])
        sides = jnp.where(lane // 2 == index, turn(value, 2 * index + 1), sides)
    unfolded[0:COLS] = sides
    lane = lanes((THIRD, 128))
    second, third = turn(unfolded[THIRD : 2 * THIRD], 40), turn(unfolded[2 * THIRD : 3 * THIRD], 80)
    side_ref[...] = jnp.where(
        lane < 40, unfolded[0:THIRD], jnp.where(lane < 80, second, third)
    )


def unfold(value):
    return jnp.concatenate([value, turn(value, -40), turn(value, -80)], axis=0)[0:COLS]


def edge(adjoint, land, diffusivity):
    return pl.pallas_call(
        edge_kernel,
        out_shape=(
            jax.ShapeDtypeStruct((24, 128), F32),
            jax.ShapeDtypeStruct((24, 128), F32),
            jax.ShapeDtypeStruct((THIRD, 128), F32),
        ),
        in_specs=[pl.BlockSpec(memory_space=pltpu.VMEM)] * 3,
        out_specs=[pl.BlockSpec(memory_space=pltpu.VMEM)] * 3,
        scratch_shapes=[pltpu.VMEM((3 * THIRD, 128), F32)],
        compiler_params=pltpu.CompilerParams(vmem_limit_bytes=24 * 2**20),
        name="edge",
    )(adjoint, land, diffusivity)


def stencil_kernel(
    adjoint_ref,
    land_ref,
    kappa_ref,
    near_side_ref,
    far_side_ref,
    out_ref,
    flow_ref,
    rim_ref,
    field,
):
    whole = (COLS, 128)
    lane = lanes(whole)
    centre, low, high = pl.ds(8, COLS), pl.ds(7, COLS), pl.ds(9, COLS)
    lat_even = even("lat")
    south_all = unfold(jnp.where(lat_even, far_side_ref[...], near_side_ref[...]))
    north_all = unfold(jnp.where(lat_even, near_side_ref[...], far_side_ref[...]))
    mask = land_ref[...].astype(F32)
    field[0:8] = jnp.zeros((8, 128), F32)
    field[136:144] = jnp.zeros((8, 128), F32)
    field[144:152] = jnp.zeros((8, 128), F32)

    def around(value, index):
        field[centre] = value
        above = jnp.where(lane == 127, turn(north_all, 126 - 2 * index), turn(value, -1))
        below = jnp.where(lane == 0, turn(south_all, -2 * index), turn(value, 1))
        return field[low], field[high], above, below

    mask_around = around(mask, 16)
    weights = []
    for number in range(2):
        kappa = kappa_ref[:, number, :]
        near = around(kappa, 17 + number)
        four = [faces(mask, kappa, m, k) for m, k in zip(mask_around, near)]
        weights.append((1.0 - (four[0] + four[1] + four[2] + four[3]), *four))
    pressure_mask = PRESSURE * mask
    pressure_east, pressure_north = PRESSURE * mask_around[1], PRESSURE * mask_around[2]

    for level in range(4):
        density = None
        for name in range(4):
            own, *four = weights[name // 2]
            tilde = adjoint_ref[level_rows(name, level)] * mask
            near = around(tilde, 4 * name + level)
            total = own * tilde
            for weight, value in zip(four, near):
                total = total + weight * value
            if name == 0:
                density = pressure_east * tilde - pressure_mask * near[0]
            elif name == 1:
                density = density + pressure_north * tilde - pressure_mask * near[3]
            elif name == 2:
                total = total - ALPHA_T * density
            else:
                total = total + BETA_S * density
            if name < 2:
                flow_ref[level_rows(name, level)] = total
            else:
                out_ref[level_rows(name - 2, level)] = total
    for number, start in enumerate(RIM):
        rim_ref[8 * number : 8 * number + 8] = out_ref[start : start + 8]


def stencil(adjoint, land, diffusivity, near_side, far_side):
    return pl.pallas_call(
        stencil_kernel,
        grid=(1,),
        out_shape=(
            jax.ShapeDtypeStruct(adjoint.shape, F32),
            jax.ShapeDtypeStruct((2 * FIELD, 128), F32),
            jax.ShapeDtypeStruct((24, 128), F32),
        ),
        in_specs=[pl.BlockSpec(memory_space=pltpu.VMEM)] * 5,
        out_specs=[
            pl.BlockSpec((2 * FIELD, 128), lambda i: (1, 0)),
            pl.BlockSpec(memory_space=pltpu.VMEM),
            pl.BlockSpec(memory_space=pltpu.VMEM),
        ],
        scratch_shapes=[pltpu.VMEM((152, 128), F32)],
        compiler_params=pltpu.CompilerParams(vmem_limit_bytes=24 * 2**20),
        name="stencil",
    )(adjoint, land, diffusivity, near_side, far_side)


def crossing(own_near, own_far, near, far):
    lon_even = even("lon")
    own_west, own_east = jnp.where(lon_even, own_far, own_near), jnp.where(lon_even, own_near, own_far)
    west, east = jnp.where(lon_even, far, near), jnp.where(lon_even, near, far)

    def flux(own, other):
        masks = own[16:17] * other[16:17]
        first, second = (0.5 * (own[k : k + 1] + other[k : k + 1]) * masks for k in (17, 18))
        step = other[0:16] - own[0:16]
        return first * step[0:8], second * step[8:16]

    west_flow, west_tracer = flux(own_west, west)
    east_flow, east_tracer = flux(own_east, east)
    west_density = -PRESSURE * own_west[16:17] * west[0:4]
    east_density = PRESSURE * east[16:17] * own_east[0:4]
    west_tracer += jnp.concatenate([-ALPHA_T * west_density, BETA_S * west_density], axis=0)
    east_tracer += jnp.concatenate([-ALPHA_T * east_density, BETA_S * east_density], axis=0)
    return west_flow, east_flow, west_tracer, east_tracer


def remove_kernel(
    chunks_ref,
    flow_ref,
    rim_ref,
    own_near_ref,
    own_far_ref,
    near_ref,
    far_ref,
    whole_ref,
    out_ref,
    new_flow,
    new_rim,
    high,
    done,
):
    del whole_ref
    west, east, west_tracer, east_tracer = crossing(
        own_near_ref[...], own_far_ref[...], near_ref[...], far_ref[...]
    )
    none = jnp.zeros((4, 128), F32)
    new_rim[...] = rim_ref[...] + jnp.concatenate(
        [west_tracer[0:4], none, east_tracer[0:4], west_tracer[4:8], none, east_tracer[4:8]], axis=0
    )
    copies = [
        pltpu.make_async_copy(
            new_rim.at[pl.ds(8 * number, 8)],
            out_ref.at[pl.ds(2 * FIELD + start, 8)],
            done.at[number],
        )
        for number, start in enumerate(RIM)
    ]
    polar = at_pole()
    for copy in copies:
        copy.start()
    for name, (start, size) in enumerate(((0, FIELD - 4), (FIELD - 4, FIELD + 4))):

        @pl.when(polar)
        def _():
            remove_waves(name, chunks_ref, flow_ref, new_flow, high)

        rows = pl.ds(FIELD * name, FIELD)

        @pl.when(jnp.logical_not(polar))
        def _():
            new_flow[rows] = flow_ref[rows]

        first, last = pl.ds(FIELD * name, 4), pl.ds(FIELD * name + FIELD - 4, 4)
        new_flow[first] = new_flow[first] + west[4 * name : 4 * name + 4]
        new_flow[last] = new_flow[last] + east[4 * name : 4 * name + 4]
        rows = pl.ds(start, size)
        copy = pltpu.make_async_copy(new_flow.at[rows], out_ref.at[rows], done.at[3 + name])
        copy.start()
        copies.append(copy)
    for copy in copies:
        copy.wait()


def remove_waves(name, chunks_ref, flow_ref, out_ref, high):
    north = poles()[1]
    group, square = (8, 128), (128, 128)
    quarter_of = (lanes(group) // ROWS + sublanes(group)) % 8
    here = (lanes(square) >= 64) == north
    for level in range(0, 4, 2):
        first = 16 * name + 4 * level
        starts = [CHUNK * (first + place) for place in range(8)]
        both = jnp.concatenate([chunks_ref[a : a + ROWS].astype(F32) for a in starts], axis=0).T
        across = turn(both, 64)
        for second in range(2):
            others = jnp.zeros(group, F32)
            for quarter in range(4):
                start = starts[4 * second + quarter] + ROWS
                row = turn(chunks_ref[start : start + 2].astype(F32)[0:1], ROWS * (quarter + 1))
                others = jnp.where(quarter_of == quarter, row, others)
            others = spread(others)
            others = jnp.where(north, turn(others, 64), others)
            straight = jnp.where(north, across, both) if second == 0 else jnp.where(north, both, across)
            high[1:129] = jnp.where(here, straight, 0.0)
            high[0:1] = others[0:1]
            high[129:135] = others[1:7]
            rows_of = level_rows(name, level + second)
            out_ref[rows_of] = flow_ref[rows_of] - high[0:COLS]


def remove(chunks, flow, rim, own_near, own_far, near, far, whole):
    return pl.pallas_call(
        remove_kernel,
        out_shape=jax.ShapeDtypeStruct(whole.shape, F32),
        in_specs=[pl.BlockSpec(memory_space=pltpu.VMEM)] * 7 + [pl.BlockSpec(memory_space=pl.ANY)],
        out_specs=pl.BlockSpec(memory_space=pl.ANY),
        scratch_shapes=[
            pltpu.VMEM((2 * FIELD, 128), F32),
            pltpu.VMEM((24, 128), F32),
            pltpu.VMEM((136, 128), F32),
            pltpu.SemaphoreType.DMA((5,)),
        ],
        input_output_aliases={7: 0},
        compiler_params=pltpu.CompilerParams(vmem_limit_bytes=24 * 2**20),
        name="remove",
    )(chunks, flow, rim, own_near, own_far, near, far, whole)


def swap(value, axis, first):
    count = lax.axis_size(axis)
    pairs = []
    for a in range(first, count, 2):
        b = a + 1
        if b == count:
            if axis == "lat":
                continue
            b = 0
        pairs += [(a, b), (b, a)]
    return lax.ppermute(value, axis, pairs)


def exchange(chunks):
    pairs = chunks.reshape(-1, 2, chunks.shape[1])
    return lax.all_to_all(pairs, "lon", split_axis=0, concat_axis=0, tiled=True).reshape(chunks.shape)


def local(adjoint, land, diffusivity, cutoff):
    lon_index, lat_index = lax.axis_index("lon"), lax.axis_index("lat")
    first_cut = jnp.where(lat_index == lax.axis_size("lat") - 1, PROWS, 0) + lon_index % 4 * ROWS
    cuts = lax.dynamic_slice_in_dim(cutoff, first_cut, ROWS, 0)
    square = jnp.broadcast_to(jnp.square(cuts.astype(F32))[:, None], (ROWS, 128))

    shape = adjoint.shape
    fields = jnp.transpose(adjoint, (0, 2, 1, 3)).reshape(-1, shape[3])
    kappas = jnp.transpose(diffusivity, (1, 0, 2))

    chunks = pack(fields, land, kappas)
    circles = exchange(chunks)
    own_near, own_far, sides = edge(fields, land, kappas)
    near_side = swap(sides, "lat", 0)
    far_side = swap(sides, "lat", 1)
    circles, near_side, far_side = lax.optimization_barrier((circles, near_side, far_side))

    filtered = filter_rows(circles, square)
    filtered, own_near, own_far = lax.optimization_barrier((filtered, own_near, own_far))
    removed = exchange(filtered)
    near = swap(own_near, "lon", 0)
    far = swap(own_far, "lon", 1)
    whole, flow, rim = stencil(fields, land, kappas, near_side, far_side)

    out = remove(removed, flow, rim, own_near, own_far, near, far, whole)
    return jnp.transpose(out.reshape(shape[0], shape[2], shape[1], shape[3]), (0, 2, 1, 3))


def solution(mesh):
    placed = (P(None, None, "lon", "lat"), P("lon", "lat"), P(None, "lon", "lat"), P())
    return jax.shard_map(
        local, mesh=mesh, in_specs=placed, out_specs=P(None, None, "lon", "lat"), check_vma=False
    )
```

```python
import math

import jax
import jax.numpy as jnp
import numpy as np
from jax import lax
from jax.experimental import pallas as pl
from jax.experimental.pallas import tpu as pltpu
from jax.sharding import PartitionSpec as P

PROWS = 64
PRESSURE = 0.3
ALPHA_T = 1.0
BETA_S = 0.8

RING = 32
COLS = 135
NLON = RING * COLS
INV = 23
CRT_RING = 3105
CRT_COLS = 1216
WAVES = 68
ROWS = 16
LEVELS = 4
FIELD = COLS * LEVELS
RIM = (0, FIELD - 4, 2 * FIELD - 8)
CHUNK = ROWS + 2
THIRD = 48
PART = 8 * CHUNK

MAIN = [lane + 1 for lane in range(128)]
EXTRA = [0] + list(range(129, 135)) + [None]

F32 = jnp.float32
BF16 = jnp.bfloat16


def tables():
    waves = np.arange(WAVES)

    def transform(slots):
        columns = MAIN + [column for column in slots for _ in range(ROWS)]
        used = np.array([[float(column is not None)] for column in columns])
        order = np.array([[column or 0] for column in columns])
        angle = 2.0 * math.pi * ((38 * order * waves) % COLS) / COLS
        table = np.zeros((256, 256))
        table[:, :WAVES] = np.cos(angle) * used
        table[:, 128 : 128 + WAVES] = -np.sin(angle) * used
        return table

    forward, backward = transform(EXTRA), transform(EXTRA[::-1]).T
    backward *= np.where(np.arange(256) % 128 == 0, 1.0, 2.0)[:, None]
    inverse_square = np.ones((RING, 128))
    for place in range(RING):
        kappa = int(format(place, "05b")[::-1], 2)
        ring_wave = 7 * kappa % RING
        k = (CRT_RING * ring_wave + CRT_COLS * waves) % NLON
        k = np.minimum(k, NLON - k)
        inverse_square[place, :WAVES] = np.where(k == 0, 1e6, 1.0 / np.maximum(k, 1) ** 2)
    return (
        jnp.asarray(forward, BF16),
        jnp.asarray(backward, BF16),
        jnp.asarray(inverse_square, F32),
    )


def turn(value, shift):
    size = value.shape[-1]
    shift %= size
    return value if shift == 0 else pltpu.roll(value, shift, value.ndim - 1)


def lanes(shape):
    return lax.broadcasted_iota(jnp.int32, shape, len(shape) - 1)


def sublanes(shape):
    return lax.broadcasted_iota(jnp.int32, shape, len(shape) - 2)


def level_rows(field, level):
    return pl.ds(FIELD * field + level, COLS, stride=LEVELS)


def faces(mask, kappa, mask_near, kappa_near):
    return 0.5 * (kappa + kappa_near) * mask * mask_near


def poles():
    index = lax.axis_index("lat")
    return index == 0, index == lax.axis_size("lat") - 1


def at_pole():
    south, north = poles()
    return jnp.logical_or(south, north)


def even(axis):
    return lax.axis_index(axis) % 2 == 0


def clear_ends(field):
    for place in range(field.shape[0]):
        field[place, 0:8] = jnp.zeros((8, 128), F32)
        field[place, 136:144] = jnp.zeros((8, 128), F32)


def spread(value):
    return pltpu.roll(value, 0, 1, stride=ROWS, stride_axis=0)


def pack_kernel(*refs):
    @pl.when(at_pole())
    def _():
        pack_rows(*refs)


def pack_rows(
    adjoint_hbm, land_hbm, kappa_hbm, out_hbm, rows, land, kappas, field, part, chunks, arrived, left
):
    def arrival(source, target, number):
        copy = pltpu.make_async_copy(source, target, arrived.at[number])
        copy.start()
        return copy

    first = arrival(land_hbm, land, 0), arrival(kappa_hbm, kappas, 1)
    half = FIELD + 4
    fields = [
        arrival(adjoint_hbm.at[pl.ds(start, size)], rows.at[pl.ds(start, size)], number)
        for number, start, size in ((2, 0, half), (3, half, 2 * FIELD - half))
    ]
    north = poles()[1]
    whole = (COLS, 128)
    low, high = pl.ds(7, COLS), pl.ds(9, COLS)
    centre = pl.ds(8, COLS)
    clear_ends(field)
    lane = lanes(whole)
    chosen = (lanes((PROWS, 128)) == sublanes((PROWS, 128)) + jnp.where(north, 64, 0)).astype(BF16)
    group = (8, 128)
    slot = sublanes(group)
    in_slot = lanes(group) // ROWS == slot

    for copy in first:
        copy.wait()
    mask = land[...].astype(F32)
    kappa = kappas[:, 0, :]
    field[0, centre] = kappa
    kappa_west, kappa_east = field[0, low], field[0, high]
    field[1, centre] = mask
    mask_west, mask_east = field[1, low], field[1, high]
    west = faces(mask, kappa, mask_west, kappa_west)
    east = faces(mask, kappa, mask_east, kappa_east)
    up = faces(mask, kappa, jnp.where(lane == 127, 0.0, turn(mask, -1)), turn(kappa, -1))
    down = faces(mask, kappa, jnp.where(lane == 0, 0.0, turn(mask, 1)), turn(kappa, 1))
    own = 1.0 - (west + east + up + down)
    edge_fixed = jnp.zeros(group, F32)
    for place, row in ((1, kappa[134:135]), (2, mask[134:135]), (4, kappa[0:1]), (5, mask[0:1])):
        edge_fixed = jnp.where(slot == place, row, edge_fixed)

    copies = []
    for name in range(2):
        fields[name].wait()
        for level in range(4):
            tilde = rows[level_rows(name, level)] * mask
            place = 2 + 4 * name + level
            field[place, centre] = tilde
            partial = (
                own * tilde
                + west * field[place, low]
                + east * field[place, high]
                + up * turn(tilde, -1)
                + down * turn(tilde, 1)
            )
            part[place, pl.ds(7, COLS)] = partial
            turned = lax.dot_general(
                chosen,
                part[place, 8:136].astype(BF16),
                (((1,), (1,)), ((), ())),
                preferred_element_type=F32,
            ).astype(BF16)
            others = jnp.where(slot == 0, partial[0:1], part[place, pl.ds(135, 8)])
            others = jnp.where(slot == 7, 0.0, others)
            edges = jnp.where(slot == 0, tilde[134:135], jnp.where(slot == 3, tilde[0:1], edge_fixed))
            others = spread(jnp.where(north, turn(others, 64), others))
            edges = spread(jnp.where(north, turn(edges, 64), edges))
            for quarter in range(4):
                place = CHUNK * (16 * name + 4 * level + quarter)
                chunks[place : place + ROWS] = turned[ROWS * quarter : ROWS * quarter + ROWS]
                two = [
                    jnp.sum(
                        jnp.where(in_slot, turn(value, -ROWS * quarter), 0.0), axis=0, keepdims=True
                    )
                    for value in (others, edges)
                ]
                chunks[place + ROWS : place + CHUNK] = jnp.concatenate(two, axis=0).astype(BF16)
            if level % 2:
                number = 2 * name + level // 2
                span = pl.ds(PART * number, PART)
                copy = pltpu.make_async_copy(chunks.at[span], out_hbm.at[span], left.at[number])
                copy.start()
                copies.append(copy)
    for copy in copies:
        copy.wait()


def pack(adjoint, land, diffusivity):
    return pl.pallas_call(
        pack_kernel,
        out_shape=jax.ShapeDtypeStruct((RING * CHUNK, 128), BF16),
        in_specs=[pl.BlockSpec(memory_space=pl.ANY)] * 3,
        out_specs=pl.BlockSpec(memory_space=pl.ANY),
        scratch_shapes=[
            pltpu.VMEM((2 * FIELD, 128), F32),
            pltpu.VMEM((COLS, 128), jnp.int32),
            pltpu.VMEM((COLS, 2, 128), F32),
            pltpu.VMEM((10, 152, 128), F32),
            pltpu.VMEM((10, 144, 128), F32),
            pltpu.VMEM((RING * CHUNK, 128), BF16),
            pltpu.SemaphoreType.DMA((4,)),
            pltpu.SemaphoreType.DMA((4,)),
        ],
        compiler_params=pltpu.CompilerParams(vmem_limit_bytes=60 * 2**20),
        name="pack",
    )(adjoint, land, diffusivity)


def times(re, im, angle_index, count, sign):
    eighth = 8 * angle_index // count if 8 * angle_index % count == 0 else None
    half = math.sqrt(0.5)
    if eighth == 0:
        return re, im
    if eighth == 2:
        return (-im, re) if sign > 0 else (im, -re)
    if eighth == 1:
        if sign > 0:
            return half * (re - im), half * (re + im)
        return half * (re + im), half * (im - re)
    if eighth == 3:
        if sign > 0:
            return -half * (re + im), half * (re - im)
        return half * (im - re), -half * (re + im)
    cos = math.cos(2.0 * math.pi * angle_index / count)
    sin = sign * math.sin(2.0 * math.pi * angle_index / count)
    return cos * re - sin * im, sin * re + cos * im


def fourier(values):
    half = RING // 2
    while half:
        for start in range(0, RING, 2 * half):
            for i in range(half):
                a, b = start + i, start + i + half
                (ar, ai), (br, bi) = values[a], values[b]
                values[a] = (ar + br, ai + bi)
                values[b] = times(ar - br, ai - bi, i, 2 * half, -1)
        half //= 2


def fourier_back(values):
    half = 1
    while half < RING:
        for start in range(0, RING, 2 * half):
            for i in range(half):
                a, b = start + i, start + i + half
                ar, ai = values[a]
                br, bi = times(*values[b], i, 2 * half, 1)
                values[a] = (ar + br, ai + bi)
                values[b] = (ar - br, ai - bi)
        half *= 2


def ring_shift(value, step, columns):
    slot = lanes(value.shape) // ROWS
    for bit in range(5):
        moved = pltpu.roll(value, step * 2**bit % RING, 0)
        picked = jnp.zeros(value.shape, jnp.bool_)
        for place, column in enumerate(columns):
            if (column or 0) >> bit & 1:
                picked = jnp.logical_or(picked, slot == place)
        value = jnp.where(picked, moved, value)
    return value


def filter_kernel(*refs):
    @pl.when(at_pole())
    def _():
        filter_circles(*refs)


def filter_circles(
    in_ref, square_ref, forward_ref, backward_ref, inverse_ref, out_ref, held, wave, pair
):
    tile = (ROWS, 128)
    own_row = lanes(tile) % ROWS == sublanes(tile)
    column = lanes(tile) + 1
    rows = []
    for t in range(RING):
        start = CHUNK * (INV * t % RING)
        rows.append(in_ref[start : start + ROWS])
        pair[2 * t : 2 * t + 2] = in_ref[start + ROWS : start + CHUNK].astype(F32)
    for bit in range(5):
        picked = (column >> bit) & 1 == 1
        rows = [jnp.where(picked, rows[(t - 2**bit) % RING], rows[t]) for t in range(RING)]
    for t in range(RING):
        held[ROWS * t : ROWS * t + ROWS, 0:128] = rows[t]

    others, edges = pair[pl.ds(0, RING, stride=2)], pair[pl.ds(1, RING, stride=2)]
    slot = lanes(others.shape) // ROWS
    beyond = turn(pltpu.roll(edges, RING - 7, 0), -3 * ROWS)
    flux = (beyond - edges) * turn(0.5 * (beyond + edges), -ROWS) * turn(beyond * edges, -2 * ROWS)
    others = others + jnp.where(slot == 6, turn(flux, 6 * ROWS), 0.0)
    others = others - jnp.where(slot == 0, pltpu.roll(flux, 7, 0), 0.0)
    pair[0:RING] = ring_shift(others, 1, EXTRA)
    for t in range(RING):
        side = jnp.where(own_row, pair[t : t + 1], 0.0)
        held[ROWS * t : ROWS * t + ROWS, 128:256] = side.astype(BF16)

    wave[...] = jnp.dot(held[...], forward_ref[...], preferred_element_type=F32)
    for half in range(2):
        rows_of = [pl.ds(ROWS * t + 8 * half, 8) for t in range(RING)]
        values = [(wave[r, 0:128], wave[r, 128:256]) for r in rows_of]
        fourier(values)
        square = square_ref[8 * half : 8 * half + 8]
        for t in range(RING):
            keep = jnp.maximum(0.0, 1.0 - square * inverse_ref[t : t + 1]) * (1.0 / NLON)
            values[t] = (values[t][0] * keep, values[t][1] * keep)
        fourier_back(values)
        for t in range(RING):
            wave[rows_of[t], 0:128] = values[t][0]
            wave[rows_of[t], 128:256] = values[t][1]
    wave[...] = jnp.dot(wave[...].astype(BF16), backward_ref[...], preferred_element_type=F32)

    for t in range(RING):
        side = jnp.where(own_row, wave[ROWS * t : ROWS * t + ROWS, 128:256], 0.0)
        held[ROWS * t : ROWS * t + ROWS, 128:256] = side.astype(BF16)
    shape = (RING, RING * ROWS)
    gather = (lanes(shape) // ROWS == sublanes(shape)).astype(BF16)
    others = jnp.dot(gather, held[:, 128:256], preferred_element_type=F32)
    pair[0:RING] = ring_shift(others, -1, EXTRA[::-1])

    rows = [wave[ROWS * t : ROWS * t + ROWS, 0:128].astype(BF16) for t in range(RING)]
    for bit in range(5):
        picked = (column >> bit) & 1 == 1
        rows = [jnp.where(picked, rows[(t + 2**bit) % RING], rows[t]) for t in range(RING)]
    for d in range(RING):
        place = 7 * d % RING
        out_ref[CHUNK * d : CHUNK * d + ROWS] = rows[place]
        last = jnp.broadcast_to(pair[place : place + 1], (2, 128))
        out_ref[CHUNK * d + ROWS : CHUNK * d + CHUNK] = last.astype(BF16)


def filter_rows(chunks, square):
    forward, backward, inverse_square = tables()
    return pl.pallas_call(
        filter_kernel,
        out_shape=jax.ShapeDtypeStruct((RING * CHUNK, 128), BF16),
        in_specs=[pl.BlockSpec(memory_space=pltpu.VMEM)] * 5,
        out_specs=pl.BlockSpec(memory_space=pltpu.VMEM),
        scratch_shapes=[
            pltpu.VMEM((RING * ROWS, 256), BF16),
            pltpu.VMEM((RING * ROWS, 256), F32),
            pltpu.VMEM((2 * RING, 128), F32),
        ],
        compiler_params=pltpu.CompilerParams(vmem_limit_bytes=24 * 2**20),
        name="filter",
    )(chunks, square, forward, backward, inverse_square)


def edge_kernel(adjoint_ref, land_ref, kappa_ref, near_ref, far_ref, side_ref, unfolded):
    lon_even = even("lon")
    whole = (COLS, 128)
    lane = lanes(whole)
    mask = land_ref[...].astype(F32)
    sides = jnp.zeros(whole, F32)
    near_ref[...] = jnp.zeros((24, 128), F32)
    far_ref[...] = jnp.zeros((24, 128), F32)
    for index in range(19):
        if index < 16:
            value = adjoint_ref[level_rows(index // 4, index % 4)] * mask
        elif index == 16:
            value = mask
        else:
            value = kappa_ref[:, index - 17, :]
        near_ref[index : index + 1] = jnp.where(lon_even, value[134:135], value[0:1])
        far_ref[index : index + 1] = jnp.where(lon_even, value[0:1], value[134:135])
        sides = jnp.where(lane // 2 == index, turn(value, 2 * index + 1), sides)
    unfolded[0:COLS] = sides
    lane = lanes((THIRD, 128))
    second, third = turn(unfolded[THIRD : 2 * THIRD], 40), turn(unfolded[2 * THIRD : 3 * THIRD], 80)
    side_ref[...] = jnp.where(
        lane < 40, unfolded[0:THIRD], jnp.where(lane < 80, second, third)
    )


def unfold(value):
    return jnp.concatenate([value, turn(value, -40), turn(value, -80)], axis=0)[0:COLS]


def edge(adjoint, land, diffusivity):
    return pl.pallas_call(
        edge_kernel,
        out_shape=(
            jax.ShapeDtypeStruct((24, 128), F32),
            jax.ShapeDtypeStruct((24, 128), F32),
            jax.ShapeDtypeStruct((THIRD, 128), F32),
        ),
        in_specs=[pl.BlockSpec(memory_space=pltpu.VMEM)] * 3,
        out_specs=[pl.BlockSpec(memory_space=pltpu.VMEM)] * 3,
        scratch_shapes=[pltpu.VMEM((3 * THIRD, 128), F32)],
        compiler_params=pltpu.CompilerParams(vmem_limit_bytes=24 * 2**20),
        name="edge",
    )(adjoint, land, diffusivity)


def stencil_kernel(
    adjoint_ref,
    land_ref,
    kappa_ref,
    near_side_ref,
    far_side_ref,
    out_ref,
    flow_ref,
    rim_ref,
    field,
):
    whole = (COLS, 128)
    lane = lanes(whole)
    centre, low, high = pl.ds(8, COLS), pl.ds(7, COLS), pl.ds(9, COLS)
    lat_even = even("lat")
    south_all = unfold(jnp.where(lat_even, far_side_ref[...], near_side_ref[...]))
    north_all = unfold(jnp.where(lat_even, near_side_ref[...], far_side_ref[...]))
    halos = jnp.where(lane % 2 == 0, south_all, turn(north_all, -2))
    mask = land_ref[...].astype(F32)
    clear_ends(field)

    def around(value, index):
        field[index, centre] = value
        halo = turn(halos, -2 * index)
        above = jnp.where(lane == 127, halo, turn(value, -1))
        below = jnp.where(lane == 0, halo, turn(value, 1))
        return field[index, low], field[index, high], above, below

    mask_around = around(mask, 16)
    weights = []
    for number in range(2):
        kappa = kappa_ref[:, number, :]
        near = around(kappa, 17 + number)
        four = [faces(mask, kappa, m, k) for m, k in zip(mask_around, near)]
        weights.append((1.0 - (four[0] + four[1] + four[2] + four[3]), *four))
    pressure_mask = PRESSURE * mask
    pressure_east, pressure_north = PRESSURE * mask_around[1], PRESSURE * mask_around[2]

    for level in range(4):
        density = None
        for name in range(4):
            own, *four = weights[name // 2]
            tilde = adjoint_ref[level_rows(name, level)] * mask
            near = around(tilde, 4 * name + level)
            total = own * tilde
            for weight, value in zip(four, near):
                total = total + weight * value
            if name == 0:
                density = pressure_east * tilde - pressure_mask * near[0]
            elif name == 1:
                density = density + pressure_north * tilde - pressure_mask * near[3]
            elif name == 2:
                total = total - ALPHA_T * density
            else:
                total = total + BETA_S * density
            if name < 2:
                flow_ref[level_rows(name, level)] = total
            else:
                out_ref[level_rows(name - 2, level)] = total
    for number, start in enumerate(RIM):
        rim_ref[8 * number : 8 * number + 8] = out_ref[start : start + 8]


def stencil(adjoint, land, diffusivity, near_side, far_side):
    return pl.pallas_call(
        stencil_kernel,
        grid=(1,),
        out_shape=(
            jax.ShapeDtypeStruct(adjoint.shape, F32),
            jax.ShapeDtypeStruct((2 * FIELD, 128), F32),
            jax.ShapeDtypeStruct((24, 128), F32),
        ),
        in_specs=[pl.BlockSpec(memory_space=pltpu.VMEM)] * 5,
        out_specs=[
            pl.BlockSpec((2 * FIELD, 128), lambda i: (1, 0)),
            pl.BlockSpec(memory_space=pltpu.VMEM),
            pl.BlockSpec(memory_space=pltpu.VMEM),
        ],
        scratch_shapes=[pltpu.VMEM((19, 152, 128), F32)],
        compiler_params=pltpu.CompilerParams(vmem_limit_bytes=24 * 2**20),
        name="stencil",
    )(adjoint, land, diffusivity, near_side, far_side)


def crossing(own_near, own_far, near, far):
    lon_even = even("lon")
    own_west, own_east = jnp.where(lon_even, own_far, own_near), jnp.where(lon_even, own_near, own_far)
    west, east = jnp.where(lon_even, far, near), jnp.where(lon_even, near, far)

    def flux(own, other):
        masks = own[16:17] * other[16:17]
        first, second = (0.5 * (own[k : k + 1] + other[k : k + 1]) * masks for k in (17, 18))
        step = other[0:16] - own[0:16]
        return first * step[0:8], second * step[8:16]

    west_flow, west_tracer = flux(own_west, west)
    east_flow, east_tracer = flux(own_east, east)
    west_density = -PRESSURE * own_west[16:17] * west[0:4]
    east_density = PRESSURE * east[16:17] * own_east[0:4]
    west_tracer += jnp.concatenate([-ALPHA_T * west_density, BETA_S * west_density], axis=0)
    east_tracer += jnp.concatenate([-ALPHA_T * east_density, BETA_S * east_density], axis=0)
    return west_flow, east_flow, west_tracer, east_tracer


def remove_kernel(
    chunks_ref,
    flow_ref,
    rim_ref,
    own_near_ref,
    own_far_ref,
    near_ref,
    far_ref,
    whole_ref,
    out_ref,
    new_flow,
    new_rim,
    high,
    done,
):
    del whole_ref
    west, east, west_tracer, east_tracer = crossing(
        own_near_ref[...], own_far_ref[...], near_ref[...], far_ref[...]
    )
    none = jnp.zeros((4, 128), F32)
    new_rim[...] = rim_ref[...] + jnp.concatenate(
        [west_tracer[0:4], none, east_tracer[0:4], west_tracer[4:8], none, east_tracer[4:8]], axis=0
    )
    copies = [
        pltpu.make_async_copy(
            new_rim.at[pl.ds(8 * number, 8)],
            out_ref.at[pl.ds(2 * FIELD + start, 8)],
            done.at[number],
        )
        for number, start in enumerate(RIM)
    ]
    polar = at_pole()
    for copy in copies:
        copy.start()
    for name, (start, size) in enumerate(((0, FIELD - 4), (FIELD - 4, FIELD + 4))):

        @pl.when(polar)
        def _():
            remove_waves(name, chunks_ref, flow_ref, new_flow, high)

        rows = pl.ds(FIELD * name, FIELD)

        @pl.when(jnp.logical_not(polar))
        def _():
            new_flow[rows] = flow_ref[rows]

        first, last = pl.ds(FIELD * name, 4), pl.ds(FIELD * name + FIELD - 4, 4)
        new_flow[first] = new_flow[first] + west[4 * name : 4 * name + 4]
        new_flow[last] = new_flow[last] + east[4 * name : 4 * name + 4]
        rows = pl.ds(start, size)
        copy = pltpu.make_async_copy(new_flow.at[rows], out_ref.at[rows], done.at[3 + name])
        copy.start()
        copies.append(copy)
    for copy in copies:
        copy.wait()


def remove_waves(name, chunks_ref, flow_ref, out_ref, high):
    north = poles()[1]
    group, square = (8, 128), (128, 128)
    quarter_of = (lanes(group) // ROWS + sublanes(group)) % 8
    here = (lanes(square) >= 64) == north
    for level in range(0, 4, 2):
        first = 16 * name + 4 * level
        starts = [CHUNK * (first + place) for place in range(8)]
        both = jnp.concatenate([chunks_ref[a : a + ROWS].astype(F32) for a in starts], axis=0).T
        across = turn(both, 64)
        for second in range(2):
            others = jnp.zeros(group, F32)
            for quarter in range(4):
                start = starts[4 * second + quarter] + ROWS
                row = turn(chunks_ref[start : start + 2].astype(F32)[0:1], ROWS * (quarter + 1))
                others = jnp.where(quarter_of == quarter, row, others)
            others = spread(others)
            others = jnp.where(north, turn(others, 64), others)
            straight = jnp.where(north, across, both) if second == 0 else jnp.where(north, both, across)
            place = level + second
            high[place, 1:129] = jnp.where(here, straight, 0.0)
            high[place, 0:1] = others[0:1]
            high[place, 129:135] = others[1:7]
            rows_of = level_rows(name, place)
            out_ref[rows_of] = flow_ref[rows_of] - high[place, 0:COLS]


def remove(chunks, flow, rim, own_near, own_far, near, far, whole):
    return pl.pallas_call(
        remove_kernel,
        out_shape=jax.ShapeDtypeStruct(whole.shape, F32),
        in_specs=[pl.BlockSpec(memory_space=pltpu.VMEM)] * 7 + [pl.BlockSpec(memory_space=pl.ANY)],
        out_specs=pl.BlockSpec(memory_space=pl.ANY),
        scratch_shapes=[
            pltpu.VMEM((2 * FIELD, 128), F32),
            pltpu.VMEM((24, 128), F32),
            pltpu.VMEM((4, 136, 128), F32),
            pltpu.SemaphoreType.DMA((5,)),
        ],
        input_output_aliases={7: 0},
        compiler_params=pltpu.CompilerParams(vmem_limit_bytes=24 * 2**20),
        name="remove",
    )(chunks, flow, rim, own_near, own_far, near, far, whole)


def swap(value, axis, first):
    count = lax.axis_size(axis)
    pairs = []
    for a in range(first, count, 2):
        b = a + 1
        if b == count:
            if axis == "lat":
                continue
            b = 0
        pairs += [(a, b), (b, a)]
    return lax.ppermute(value, axis, pairs)


def exchange(chunks):
    pairs = chunks.reshape(-1, 2, chunks.shape[1])
    return lax.all_to_all(pairs, "lon", split_axis=0, concat_axis=0, tiled=True).reshape(chunks.shape)


def local(adjoint, land, diffusivity, cutoff):
    lon_index, lat_index = lax.axis_index("lon"), lax.axis_index("lat")
    first_cut = jnp.where(lat_index == lax.axis_size("lat") - 1, PROWS, 0) + lon_index % 4 * ROWS
    cuts = lax.dynamic_slice_in_dim(cutoff, first_cut, ROWS, 0)
    square = jnp.broadcast_to(jnp.square(cuts.astype(F32))[:, None], (ROWS, 128))

    shape = adjoint.shape
    fields = jnp.transpose(adjoint, (0, 2, 1, 3)).reshape(-1, shape[3])
    kappas = jnp.transpose(diffusivity, (1, 0, 2))

    filtered = filter_rows(exchange(pack(fields, land, kappas)), square)
    filtered, fields, land, kappas = lax.optimization_barrier((filtered, fields, land, kappas))
    removed = exchange(filtered)
    own_near, own_far, sides = edge(fields, land, kappas)
    far_side = swap(sides, "lat", 1)
    near_side = swap(sides, "lat", 0)
    near = swap(own_near, "lon", 0)
    far = swap(own_far, "lon", 1)
    whole, flow, rim = stencil(fields, land, kappas, near_side, far_side)

    out = remove(removed, flow, rim, own_near, own_far, near, far, whole)
    return jnp.transpose(out.reshape(shape[0], shape[2], shape[1], shape[3]), (0, 2, 1, 3))


def solution(mesh):
    placed = (P(None, None, "lon", "lat"), P("lon", "lat"), P(None, "lon", "lat"), P())
    return jax.shard_map(
        local, mesh=mesh, in_specs=placed, out_specs=P(None, None, "lon", "lat"), check_vma=False
    )
```

```python
import math

import jax
import jax.numpy as jnp
import numpy as np
from jax import lax
from jax.experimental import pallas as pl
from jax.experimental.pallas import tpu as pltpu
from jax.sharding import PartitionSpec as P

PROWS = 64
PRESSURE = 0.3
ALPHA_T = 1.0
BETA_S = 0.8

RING = 32
COLS = 135
NLON = RING * COLS
INV = 23
CRT_RING = 3105
CRT_COLS = 1216
LEAD_OUT = 24
LEAD_BACK = 16
WAVES = 68
ROWS = 16
LEVELS = 4
FIELD = COLS * LEVELS
RIM = (0, FIELD - 4, 2 * FIELD - 8)
CHUNK = ROWS + 2
THIRD = 48
PART = 8 * CHUNK

MAIN = [lane + 1 for lane in range(128)]
EXTRA = [0] + list(range(129, 135)) + [None]

F32 = jnp.float32
BF16 = jnp.bfloat16


def tables():
    waves = np.arange(WAVES)

    def transform(slots):
        columns = MAIN + [column for column in slots for _ in range(ROWS)]
        used = np.array([[float(column is not None)] for column in columns])
        order = np.array([[column or 0] for column in columns])
        angle = 2.0 * math.pi * ((38 * order * waves) % COLS) / COLS
        table = np.zeros((256, 256))
        table[:, :WAVES] = np.cos(angle) * used
        table[:, 128 : 128 + WAVES] = -np.sin(angle) * used
        return table

    forward, backward = transform(EXTRA), transform(EXTRA[::-1]).T
    backward *= np.where(np.arange(256) % 128 == 0, 1.0, 2.0)[:, None]
    inverse_square = np.ones((RING, 128))
    for place in range(RING):
        kappa = int(format(place, "05b")[::-1], 2)
        ring_wave = 7 * kappa % RING
        k = (CRT_RING * ring_wave + CRT_COLS * waves) % NLON
        k = np.minimum(k, NLON - k)
        inverse_square[place, :WAVES] = np.where(k == 0, 1e6, 1.0 / np.maximum(k, 1) ** 2)
    return (
        jnp.asarray(forward, BF16),
        jnp.asarray(backward, BF16),
        jnp.asarray(inverse_square, F32),
    )


def chunk_row(tile, lead):
    return CHUNK * ((tile - lead) % RING)


def turn(value, shift):
    size = value.shape[-1]
    shift %= size
    return value if shift == 0 else pltpu.roll(value, shift, value.ndim - 1)


def lanes(shape):
    return lax.broadcasted_iota(jnp.int32, shape, len(shape) - 1)


def sublanes(shape):
    return lax.broadcasted_iota(jnp.int32, shape, len(shape) - 2)


def level_rows(field, level):
    return pl.ds(FIELD * field + level, COLS, stride=LEVELS)


def faces(mask, kappa, mask_near, kappa_near):
    return 0.5 * (kappa + kappa_near) * mask * mask_near


def poles():
    index = lax.axis_index("lat")
    return index == 0, index == lax.axis_size("lat") - 1


def at_pole():
    south, north = poles()
    return jnp.logical_or(south, north)


def even(axis):
    return lax.axis_index(axis) % 2 == 0


def clear_ends(field):
    for place in range(field.shape[0]):
        field[place, 0:8] = jnp.zeros((8, 128), F32)
        field[place, 136:144] = jnp.zeros((8, 128), F32)


def spread(value):
    return pltpu.roll(value, 0, 1, stride=ROWS, stride_axis=0)


def pack_kernel(*refs):
    @pl.when(at_pole())
    def _():
        pack_rows(*refs)


def pack_rows(
    adjoint_hbm, land_hbm, kappa_hbm, out_hbm, rows, land, kappas, field, part, chunks, arrived, left
):
    def arrival(source, target, number):
        copy = pltpu.make_async_copy(source, target, arrived.at[number])
        copy.start()
        return copy

    first = arrival(land_hbm, land, 0), arrival(kappa_hbm, kappas, 1)
    half = FIELD + 4
    fields = [
        arrival(adjoint_hbm.at[pl.ds(start, size)], rows.at[pl.ds(start, size)], number)
        for number, start, size in ((2, 0, half), (3, half, 2 * FIELD - half))
    ]
    north = poles()[1]
    whole = (COLS, 128)
    low, high = pl.ds(7, COLS), pl.ds(9, COLS)
    centre = pl.ds(8, COLS)
    clear_ends(field)
    lane = lanes(whole)
    chosen = (lanes((PROWS, 128)) == sublanes((PROWS, 128)) + jnp.where(north, 64, 0)).astype(BF16)
    group = (8, 128)
    slot = sublanes(group)
    in_slot = lanes(group) // ROWS == slot

    for copy in first:
        copy.wait()
    mask = land[...].astype(F32)
    kappa = kappas[:, 0, :]
    field[0, centre] = kappa
    kappa_west, kappa_east = field[0, low], field[0, high]
    field[1, centre] = mask
    mask_west, mask_east = field[1, low], field[1, high]
    west = faces(mask, kappa, mask_west, kappa_west)
    east = faces(mask, kappa, mask_east, kappa_east)
    up = faces(mask, kappa, jnp.where(lane == 127, 0.0, turn(mask, -1)), turn(kappa, -1))
    down = faces(mask, kappa, jnp.where(lane == 0, 0.0, turn(mask, 1)), turn(kappa, 1))
    own = 1.0 - (west + east + up + down)
    edge_fixed = jnp.zeros(group, F32)
    for place, row in ((1, kappa[134:135]), (2, mask[134:135]), (4, kappa[0:1]), (5, mask[0:1])):
        edge_fixed = jnp.where(slot == place, row, edge_fixed)

    copies = []
    for name in range(2):
        fields[name].wait()
        for level in range(4):
            tilde = rows[level_rows(name, level)] * mask
            place = 2 + 4 * name + level
            field[place, centre] = tilde
            partial = (
                own * tilde
                + west * field[place, low]
                + east * field[place, high]
                + up * turn(tilde, -1)
                + down * turn(tilde, 1)
            )
            part[place, pl.ds(7, COLS)] = partial
            turned = lax.dot_general(
                chosen,
                part[place, 8:136].astype(BF16),
                (((1,), (1,)), ((), ())),
                preferred_element_type=F32,
            ).astype(BF16)
            others = jnp.where(slot == 0, partial[0:1], part[place, pl.ds(135, 8)])
            others = jnp.where(slot == 7, 0.0, others)
            edges = jnp.where(slot == 0, tilde[134:135], jnp.where(slot == 3, tilde[0:1], edge_fixed))
            others = spread(jnp.where(north, turn(others, 64), others))
            edges = spread(jnp.where(north, turn(edges, 64), edges))
            for quarter in range(4):
                place = chunk_row(16 * name + 4 * level + quarter, LEAD_OUT)
                chunks[place : place + ROWS] = turned[ROWS * quarter : ROWS * quarter + ROWS]
                two = [
                    jnp.sum(
                        jnp.where(in_slot, turn(value, -ROWS * quarter), 0.0), axis=0, keepdims=True
                    )
                    for value in (others, edges)
                ]
                chunks[place + ROWS : place + CHUNK] = jnp.concatenate(two, axis=0).astype(BF16)
            if level % 2:
                number = 2 * name + level // 2
                span = pl.ds(chunk_row(8 * number, LEAD_OUT), PART)
                copy = pltpu.make_async_copy(chunks.at[span], out_hbm.at[span], left.at[number])
                copy.start()
                copies.append(copy)
    for copy in copies:
        copy.wait()


def pack(adjoint, land, diffusivity):
    return pl.pallas_call(
        pack_kernel,
        out_shape=jax.ShapeDtypeStruct((RING * CHUNK, 128), BF16),
        in_specs=[pl.BlockSpec(memory_space=pl.ANY)] * 3,
        out_specs=pl.BlockSpec(memory_space=pl.ANY),
        scratch_shapes=[
            pltpu.VMEM((2 * FIELD, 128), F32),
            pltpu.VMEM((COLS, 128), jnp.int32),
            pltpu.VMEM((COLS, 2, 128), F32),
            pltpu.VMEM((10, 152, 128), F32),
            pltpu.VMEM((10, 144, 128), F32),
            pltpu.VMEM((RING * CHUNK, 128), BF16),
            pltpu.SemaphoreType.DMA((4,)),
            pltpu.SemaphoreType.DMA((4,)),
        ],
        compiler_params=pltpu.CompilerParams(vmem_limit_bytes=60 * 2**20),
        name="pack",
    )(adjoint, land, diffusivity)


def times(re, im, angle_index, count, sign):
    eighth = 8 * angle_index // count if 8 * angle_index % count == 0 else None
    half = math.sqrt(0.5)
    if eighth == 0:
        return re, im
    if eighth == 2:
        return (-im, re) if sign > 0 else (im, -re)
    if eighth == 1:
        if sign > 0:
            return half * (re - im), half * (re + im)
        return half * (re + im), half * (im - re)
    if eighth == 3:
        if sign > 0:
            return -half * (re + im), half * (re - im)
        return half * (im - re), -half * (re + im)
    cos = math.cos(2.0 * math.pi * angle_index / count)
    sin = sign * math.sin(2.0 * math.pi * angle_index / count)
    return cos * re - sin * im, sin * re + cos * im


def fourier(values):
    half = RING // 2
    while half:
        for start in range(0, RING, 2 * half):
            for i in range(half):
                a, b = start + i, start + i + half
                (ar, ai), (br, bi) = values[a], values[b]
                values[a] = (ar + br, ai + bi)
                values[b] = times(ar - br, ai - bi, i, 2 * half, -1)
        half //= 2


def fourier_back(values):
    half = 1
    while half < RING:
        for start in range(0, RING, 2 * half):
            for i in range(half):
                a, b = start + i, start + i + half
                ar, ai = values[a]
                br, bi = times(*values[b], i, 2 * half, 1)
                values[a] = (ar + br, ai + bi)
                values[b] = (ar - br, ai - bi)
        half *= 2


def ring_shift(value, step, columns):
    slot = lanes(value.shape) // ROWS
    for bit in range(5):
        moved = pltpu.roll(value, step * 2**bit % RING, 0)
        picked = jnp.zeros(value.shape, jnp.bool_)
        for place, column in enumerate(columns):
            if (column or 0) >> bit & 1:
                picked = jnp.logical_or(picked, slot == place)
        value = jnp.where(picked, moved, value)
    return value


def filter_kernel(*refs):
    @pl.when(at_pole())
    def _():
        filter_circles(*refs)


def filter_circles(
    in_ref, square_ref, forward_ref, backward_ref, inverse_ref, out_ref, held, wave, pair
):
    tile = (ROWS, 128)
    own_row = lanes(tile) % ROWS == sublanes(tile)
    column = lanes(tile) + 1
    rows = []
    for t in range(RING):
        start = chunk_row(INV * t % RING, LEAD_OUT)
        rows.append(in_ref[start : start + ROWS])
        pair[2 * t : 2 * t + 2] = in_ref[start + ROWS : start + CHUNK].astype(F32)
    for bit in range(5):
        picked = (column >> bit) & 1 == 1
        rows = [jnp.where(picked, rows[(t - 2**bit) % RING], rows[t]) for t in range(RING)]
    for t in range(RING):
        held[ROWS * t : ROWS * t + ROWS, 0:128] = rows[t]

    others, edges = pair[pl.ds(0, RING, stride=2)], pair[pl.ds(1, RING, stride=2)]
    slot = lanes(others.shape) // ROWS
    beyond = turn(pltpu.roll(edges, RING - 7, 0), -3 * ROWS)
    flux = (beyond - edges) * turn(0.5 * (beyond + edges), -ROWS) * turn(beyond * edges, -2 * ROWS)
    others = others + jnp.where(slot == 6, turn(flux, 6 * ROWS), 0.0)
    others = others - jnp.where(slot == 0, pltpu.roll(flux, 7, 0), 0.0)
    pair[0:RING] = ring_shift(others, 1, EXTRA)
    for t in range(RING):
        side = jnp.where(own_row, pair[t : t + 1], 0.0)
        held[ROWS * t : ROWS * t + ROWS, 128:256] = side.astype(BF16)

    wave[...] = jnp.dot(held[...], forward_ref[...], preferred_element_type=F32)
    for half in range(2):
        rows_of = [pl.ds(ROWS * t + 8 * half, 8) for t in range(RING)]
        values = [(wave[r, 0:128], wave[r, 128:256]) for r in rows_of]
        fourier(values)
        square = square_ref[8 * half : 8 * half + 8]
        for t in range(RING):
            keep = jnp.maximum(0.0, 1.0 - square * inverse_ref[t : t + 1]) * (1.0 / NLON)
            values[t] = (values[t][0] * keep, values[t][1] * keep)
        fourier_back(values)
        for t in range(RING):
            wave[rows_of[t], 0:128] = values[t][0]
            wave[rows_of[t], 128:256] = values[t][1]
    wave[...] = jnp.dot(wave[...].astype(BF16), backward_ref[...], preferred_element_type=F32)

    for t in range(RING):
        side = jnp.where(own_row, wave[ROWS * t : ROWS * t + ROWS, 128:256], 0.0)
        held[ROWS * t : ROWS * t + ROWS, 128:256] = side.astype(BF16)
    shape = (RING, RING * ROWS)
    gather = (lanes(shape) // ROWS == sublanes(shape)).astype(BF16)
    others = jnp.dot(gather, held[:, 128:256], preferred_element_type=F32)
    pair[0:RING] = ring_shift(others, -1, EXTRA[::-1])

    rows = [wave[ROWS * t : ROWS * t + ROWS, 0:128].astype(BF16) for t in range(RING)]
    for bit in range(5):
        picked = (column >> bit) & 1 == 1
        rows = [jnp.where(picked, rows[(t + 2**bit) % RING], rows[t]) for t in range(RING)]
    for d in range(RING):
        place = 7 * d % RING
        start = chunk_row(d, LEAD_BACK)
        out_ref[start : start + ROWS] = rows[place]
        last = jnp.broadcast_to(pair[place : place + 1], (2, 128))
        out_ref[start + ROWS : start + CHUNK] = last.astype(BF16)


def filter_rows(chunks, square):
    forward, backward, inverse_square = tables()
    return pl.pallas_call(
        filter_kernel,
        out_shape=jax.ShapeDtypeStruct((RING * CHUNK, 128), BF16),
        in_specs=[pl.BlockSpec(memory_space=pltpu.VMEM)] * 5,
        out_specs=pl.BlockSpec(memory_space=pltpu.VMEM),
        scratch_shapes=[
            pltpu.VMEM((RING * ROWS, 256), BF16),
            pltpu.VMEM((RING * ROWS, 256), F32),
            pltpu.VMEM((2 * RING, 128), F32),
        ],
        compiler_params=pltpu.CompilerParams(vmem_limit_bytes=24 * 2**20),
        name="filter",
    )(chunks, square, forward, backward, inverse_square)


def edge_kernel(adjoint_ref, land_ref, kappa_ref, near_ref, far_ref, side_ref, unfolded):
    lon_even = even("lon")
    whole = (COLS, 128)
    lane = lanes(whole)
    mask = land_ref[...].astype(F32)
    sides = jnp.zeros(whole, F32)
    near_ref[...] = jnp.zeros((24, 128), F32)
    far_ref[...] = jnp.zeros((24, 128), F32)
    for index in range(19):
        if index < 16:
            value = adjoint_ref[level_rows(index // 4, index % 4)] * mask
        elif index == 16:
            value = mask
        else:
            value = kappa_ref[:, index - 17, :]
        near_ref[index : index + 1] = jnp.where(lon_even, value[134:135], value[0:1])
        far_ref[index : index + 1] = jnp.where(lon_even, value[0:1], value[134:135])
        sides = jnp.where(lane // 2 == index, turn(value, 2 * index + 1), sides)
    unfolded[0:COLS] = sides
    lane = lanes((THIRD, 128))
    second, third = turn(unfolded[THIRD : 2 * THIRD], 40), turn(unfolded[2 * THIRD : 3 * THIRD], 80)
    side_ref[...] = jnp.where(
        lane < 40, unfolded[0:THIRD], jnp.where(lane < 80, second, third)
    )


def unfold(value):
    return jnp.concatenate([value, turn(value, -40), turn(value, -80)], axis=0)[0:COLS]


def edge(adjoint, land, diffusivity):
    return pl.pallas_call(
        edge_kernel,
        out_shape=(
            jax.ShapeDtypeStruct((24, 128), F32),
            jax.ShapeDtypeStruct((24, 128), F32),
            jax.ShapeDtypeStruct((THIRD, 128), F32),
        ),
        in_specs=[pl.BlockSpec(memory_space=pltpu.VMEM)] * 3,
        out_specs=[pl.BlockSpec(memory_space=pltpu.VMEM)] * 3,
        scratch_shapes=[pltpu.VMEM((3 * THIRD, 128), F32)],
        compiler_params=pltpu.CompilerParams(vmem_limit_bytes=24 * 2**20),
        name="edge",
    )(adjoint, land, diffusivity)


def stencil_kernel(
    adjoint_ref,
    land_ref,
    kappa_ref,
    near_side_ref,
    far_side_ref,
    out_ref,
    flow_ref,
    rim_ref,
    field,
):
    whole = (COLS, 128)
    lane = lanes(whole)
    centre, low, high = pl.ds(8, COLS), pl.ds(7, COLS), pl.ds(9, COLS)
    lat_even = even("lat")
    south_all = unfold(jnp.where(lat_even, far_side_ref[...], near_side_ref[...]))
    north_all = unfold(jnp.where(lat_even, near_side_ref[...], far_side_ref[...]))
    halos = jnp.where(lane % 2 == 0, south_all, turn(north_all, -2))
    mask = land_ref[...].astype(F32)
    clear_ends(field)

    def around(value, index):
        field[index, centre] = value
        halo = turn(halos, -2 * index)
        above = jnp.where(lane == 127, halo, turn(value, -1))
        below = jnp.where(lane == 0, halo, turn(value, 1))
        return field[index, low], field[index, high], above, below

    mask_around = around(mask, 16)
    weights = []
    for number in range(2):
        kappa = kappa_ref[:, number, :]
        near = around(kappa, 17 + number)
        four = [faces(mask, kappa, m, k) for m, k in zip(mask_around, near)]
        weights.append((1.0 - (four[0] + four[1] + four[2] + four[3]), *four))
    pressure_mask = PRESSURE * mask
    pressure_east, pressure_north = PRESSURE * mask_around[1], PRESSURE * mask_around[2]

    for level in range(4):
        density = None
        for name in range(4):
            own, *four = weights[name // 2]
            tilde = adjoint_ref[level_rows(name, level)] * mask
            near = around(tilde, 4 * name + level)
            total = own * tilde
            for weight, value in zip(four, near):
                total = total + weight * value
            if name == 0:
                density = pressure_east * tilde - pressure_mask * near[0]
            elif name == 1:
                density = density + pressure_north * tilde - pressure_mask * near[3]
            elif name == 2:
                total = total - ALPHA_T * density
            else:
                total = total + BETA_S * density
            if name < 2:
                flow_ref[level_rows(name, level)] = total
            else:
                out_ref[level_rows(name - 2, level)] = total
    for number, start in enumerate(RIM):
        rim_ref[8 * number : 8 * number + 8] = out_ref[start : start + 8]


def stencil(adjoint, land, diffusivity, near_side, far_side):
    return pl.pallas_call(
        stencil_kernel,
        grid=(1,),
        out_shape=(
            jax.ShapeDtypeStruct(adjoint.shape, F32),
            jax.ShapeDtypeStruct((2 * FIELD, 128), F32),
            jax.ShapeDtypeStruct((24, 128), F32),
        ),
        in_specs=[pl.BlockSpec(memory_space=pltpu.VMEM)] * 5,
        out_specs=[
            pl.BlockSpec((2 * FIELD, 128), lambda i: (1, 0)),
            pl.BlockSpec(memory_space=pltpu.VMEM),
            pl.BlockSpec(memory_space=pltpu.VMEM),
        ],
        scratch_shapes=[pltpu.VMEM((19, 152, 128), F32)],
        compiler_params=pltpu.CompilerParams(vmem_limit_bytes=24 * 2**20),
        name="stencil",
    )(adjoint, land, diffusivity, near_side, far_side)


def crossing(own_near, own_far, near, far):
    lon_even = even("lon")
    own_west, own_east = jnp.where(lon_even, own_far, own_near), jnp.where(lon_even, own_near, own_far)
    west, east = jnp.where(lon_even, far, near), jnp.where(lon_even, near, far)

    def flux(own, other):
        masks = own[16:17] * other[16:17]
        first, second = (0.5 * (own[k : k + 1] + other[k : k + 1]) * masks for k in (17, 18))
        step = other[0:16] - own[0:16]
        return first * step[0:8], second * step[8:16]

    west_flow, west_tracer = flux(own_west, west)
    east_flow, east_tracer = flux(own_east, east)
    west_density = -PRESSURE * own_west[16:17] * west[0:4]
    east_density = PRESSURE * east[16:17] * own_east[0:4]
    west_tracer += jnp.concatenate([-ALPHA_T * west_density, BETA_S * west_density], axis=0)
    east_tracer += jnp.concatenate([-ALPHA_T * east_density, BETA_S * east_density], axis=0)
    return west_flow, east_flow, west_tracer, east_tracer


def remove_kernel(
    chunks_ref,
    flow_ref,
    rim_ref,
    own_near_ref,
    own_far_ref,
    near_ref,
    far_ref,
    whole_ref,
    out_ref,
    new_flow,
    new_rim,
    high,
    done,
):
    del whole_ref
    west, east, west_tracer, east_tracer = crossing(
        own_near_ref[...], own_far_ref[...], near_ref[...], far_ref[...]
    )
    none = jnp.zeros((4, 128), F32)
    new_rim[...] = rim_ref[...] + jnp.concatenate(
        [west_tracer[0:4], none, east_tracer[0:4], west_tracer[4:8], none, east_tracer[4:8]], axis=0
    )
    copies = [
        pltpu.make_async_copy(
            new_rim.at[pl.ds(8 * number, 8)],
            out_ref.at[pl.ds(2 * FIELD + start, 8)],
            done.at[number],
        )
        for number, start in enumerate(RIM)
    ]
    polar = at_pole()
    for copy in copies:
        copy.start()
    for name, (start, size) in enumerate(((0, FIELD - 4), (FIELD - 4, FIELD + 4))):

        @pl.when(polar)
        def _():
            remove_waves(name, chunks_ref, flow_ref, new_flow, high)

        rows = pl.ds(FIELD * name, FIELD)

        @pl.when(jnp.logical_not(polar))
        def _():
            new_flow[rows] = flow_ref[rows]

        first, last = pl.ds(FIELD * name, 4), pl.ds(FIELD * name + FIELD - 4, 4)
        new_flow[first] = new_flow[first] + west[4 * name : 4 * name + 4]
        new_flow[last] = new_flow[last] + east[4 * name : 4 * name + 4]
        rows = pl.ds(start, size)
        copy = pltpu.make_async_copy(new_flow.at[rows], out_ref.at[rows], done.at[3 + name])
        copy.start()
        copies.append(copy)
    for copy in copies:
        copy.wait()


def remove_waves(name, chunks_ref, flow_ref, out_ref, high):
    north = poles()[1]
    group, square = (8, 128), (128, 128)
    quarter_of = (lanes(group) // ROWS + sublanes(group)) % 8
    here = (lanes(square) >= 64) == north
    for level in range(0, 4, 2):
        first = 16 * name + 4 * level
        starts = [chunk_row(first + place, LEAD_BACK) for place in range(8)]
        both = jnp.concatenate([chunks_ref[a : a + ROWS].astype(F32) for a in starts], axis=0).T
        across = turn(both, 64)
        for second in range(2):
            others = jnp.zeros(group, F32)
            for quarter in range(4):
                start = starts[4 * second + quarter] + ROWS
                row = turn(chunks_ref[start : start + 2].astype(F32)[0:1], ROWS * (quarter + 1))
                others = jnp.where(quarter_of == quarter, row, others)
            others = spread(others)
            others = jnp.where(north, turn(others, 64), others)
            straight = jnp.where(north, across, both) if second == 0 else jnp.where(north, both, across)
            place = level + second
            high[place, 1:129] = jnp.where(here, straight, 0.0)
            high[place, 0:1] = others[0:1]
            high[place, 129:135] = others[1:7]
            rows_of = level_rows(name, place)
            out_ref[rows_of] = flow_ref[rows_of] - high[place, 0:COLS]


def remove(chunks, flow, rim, own_near, own_far, near, far, whole):
    return pl.pallas_call(
        remove_kernel,
        out_shape=jax.ShapeDtypeStruct(whole.shape, F32),
        in_specs=[pl.BlockSpec(memory_space=pltpu.VMEM)] * 7 + [pl.BlockSpec(memory_space=pl.ANY)],
        out_specs=pl.BlockSpec(memory_space=pl.ANY),
        scratch_shapes=[
            pltpu.VMEM((2 * FIELD, 128), F32),
            pltpu.VMEM((24, 128), F32),
            pltpu.VMEM((4, 136, 128), F32),
            pltpu.SemaphoreType.DMA((5,)),
        ],
        input_output_aliases={7: 0},
        compiler_params=pltpu.CompilerParams(vmem_limit_bytes=24 * 2**20),
        name="remove",
    )(chunks, flow, rim, own_near, own_far, near, far, whole)


def swap(value, axis, first):
    count = lax.axis_size(axis)
    pairs = []
    for a in range(first, count, 2):
        b = a + 1
        if b == count:
            if axis == "lat":
                continue
            b = 0
        pairs += [(a, b), (b, a)]
    return lax.ppermute(value, axis, pairs)


def exchange(chunks, lead):
    pairs = chunks.reshape(-1, 2, chunks.shape[1])
    order = [[(place + lead) % RING for place in range(RING)]]
    return lax.all_to_all(
        pairs, "lon", split_axis=0, concat_axis=0, axis_index_groups=order, tiled=True
    ).reshape(chunks.shape)


def local(adjoint, land, diffusivity, cutoff):
    lon_index, lat_index = lax.axis_index("lon"), lax.axis_index("lat")
    first_cut = jnp.where(lat_index == lax.axis_size("lat") - 1, PROWS, 0) + lon_index % 4 * ROWS
    cuts = lax.dynamic_slice_in_dim(cutoff, first_cut, ROWS, 0)
    square = jnp.broadcast_to(jnp.square(cuts.astype(F32))[:, None], (ROWS, 128))

    shape = adjoint.shape
    fields = jnp.transpose(adjoint, (0, 2, 1, 3)).reshape(-1, shape[3])
    kappas = jnp.transpose(diffusivity, (1, 0, 2))

    circles = exchange(pack(fields, land, kappas), LEAD_OUT)
    own_near, own_far, sides = edge(fields, land, kappas)
    far_side = swap(sides, "lat", 1)
    near_side = swap(sides, "lat", 0)
    circles, near_side, far_side = lax.optimization_barrier((circles, near_side, far_side))

    filtered = filter_rows(circles, square)
    filtered, own_near, own_far = lax.optimization_barrier((filtered, own_near, own_far))
    removed = exchange(filtered, LEAD_BACK)
    near = swap(own_near, "lon", 0)
    far = swap(own_far, "lon", 1)
    whole, flow, rim = stencil(fields, land, kappas, near_side, far_side)

    out = remove(removed, flow, rim, own_near, own_far, near, far, whole)
    return jnp.transpose(out.reshape(shape[0], shape[2], shape[1], shape[3]), (0, 2, 1, 3))


def solution(mesh):
    placed = (P(None, None, "lon", "lat"), P("lon", "lat"), P(None, "lon", "lat"), P())
    return jax.shard_map(
        local, mesh=mesh, in_specs=placed, out_specs=P(None, None, "lon", "lat"), check_vma=False
    )
```

```python
import math

import jax
import jax.numpy as jnp
import numpy as np
from jax import lax
from jax.experimental import pallas as pl
from jax.experimental.pallas import tpu as pltpu
from jax.sharding import PartitionSpec as P

PROWS = 64
PRESSURE = 0.3
ALPHA_T = 1.0
BETA_S = 0.8

RING = 32
COLS = 135
NLON = RING * COLS
INV = 23
CRT_RING = 3105
CRT_COLS = 1216
ORDER_OUT = [(place + 24) % RING for place in range(RING)]
ORDER_BACK = [16] + [tile for tile in reversed(range(RING)) if tile != 16]
WAVES = 68
ROWS = 16
LEVELS = 4
FIELD = COLS * LEVELS
RIM = (0, FIELD - 4, 2 * FIELD - 8)
CHUNK = ROWS + 2
THIRD = 48
PART = 8 * CHUNK

MAIN = [lane + 1 for lane in range(128)]
EXTRA = [0] + list(range(129, 135)) + [None]

F32 = jnp.float32
BF16 = jnp.bfloat16


def tables():
    waves = np.arange(WAVES)

    def transform(slots):
        columns = MAIN + [column for column in slots for _ in range(ROWS)]
        used = np.array([[float(column is not None)] for column in columns])
        order = np.array([[column or 0] for column in columns])
        angle = 2.0 * math.pi * ((38 * order * waves) % COLS) / COLS
        table = np.zeros((256, 256))
        table[:, :WAVES] = np.cos(angle) * used
        table[:, 128 : 128 + WAVES] = -np.sin(angle) * used
        return table

    forward, backward = transform(EXTRA), transform(EXTRA[::-1]).T
    backward *= np.where(np.arange(256) % 128 == 0, 1.0, 2.0)[:, None]
    inverse_square = np.ones((RING, 128))
    for place in range(RING):
        kappa = int(format(place, "05b")[::-1], 2)
        ring_wave = 7 * kappa % RING
        k = (CRT_RING * ring_wave + CRT_COLS * waves) % NLON
        k = np.minimum(k, NLON - k)
        inverse_square[place, :WAVES] = np.where(k == 0, 1e6, 1.0 / np.maximum(k, 1) ** 2)
    return (
        jnp.asarray(forward, BF16),
        jnp.asarray(backward, BF16),
        jnp.asarray(inverse_square, F32),
    )


def chunk_row(tile, order):
    return CHUNK * order.index(tile)


def turn(value, shift):
    size = value.shape[-1]
    shift %= size
    return value if shift == 0 else pltpu.roll(value, shift, value.ndim - 1)


def lanes(shape):
    return lax.broadcasted_iota(jnp.int32, shape, len(shape) - 1)


def sublanes(shape):
    return lax.broadcasted_iota(jnp.int32, shape, len(shape) - 2)


def level_rows(field, level):
    return pl.ds(FIELD * field + level, COLS, stride=LEVELS)


def faces(mask, kappa, mask_near, kappa_near):
    return 0.5 * (kappa + kappa_near) * mask * mask_near


def poles():
    index = lax.axis_index("lat")
    return index == 0, index == lax.axis_size("lat") - 1


def at_pole():
    south, north = poles()
    return jnp.logical_or(south, north)


def even(axis):
    return lax.axis_index(axis) % 2 == 0


def clear_ends(field):
    for place in range(field.shape[0]):
        field[place, 0:8] = jnp.zeros((8, 128), F32)
        field[place, 136:144] = jnp.zeros((8, 128), F32)


def spread(value):
    return pltpu.roll(value, 0, 1, stride=ROWS, stride_axis=0)


def pack_kernel(*refs):
    @pl.when(at_pole())
    def _():
        pack_rows(*refs)


def pack_rows(
    adjoint_hbm, land_hbm, kappa_hbm, out_hbm, rows, land, kappas, field, part, chunks, arrived, left
):
    def arrival(source, target, number):
        copy = pltpu.make_async_copy(source, target, arrived.at[number])
        copy.start()
        return copy

    first = arrival(land_hbm, land, 0), arrival(kappa_hbm, kappas, 1)
    half = FIELD + 4
    fields = [
        arrival(adjoint_hbm.at[pl.ds(start, size)], rows.at[pl.ds(start, size)], number)
        for number, start, size in ((2, 0, half), (3, half, 2 * FIELD - half))
    ]
    north = poles()[1]
    whole = (COLS, 128)
    low, high = pl.ds(7, COLS), pl.ds(9, COLS)
    centre = pl.ds(8, COLS)
    clear_ends(field)
    lane = lanes(whole)
    chosen = (lanes((PROWS, 128)) == sublanes((PROWS, 128)) + jnp.where(north, 64, 0)).astype(BF16)
    group = (8, 128)
    slot = sublanes(group)
    in_slot = lanes(group) // ROWS == slot

    for copy in first:
        copy.wait()
    mask = land[...].astype(F32)
    kappa = kappas[:, 0, :]
    field[0, centre] = kappa
    kappa_west, kappa_east = field[0, low], field[0, high]
    field[1, centre] = mask
    mask_west, mask_east = field[1, low], field[1, high]
    west = faces(mask, kappa, mask_west, kappa_west)
    east = faces(mask, kappa, mask_east, kappa_east)
    up = faces(mask, kappa, jnp.where(lane == 127, 0.0, turn(mask, -1)), turn(kappa, -1))
    down = faces(mask, kappa, jnp.where(lane == 0, 0.0, turn(mask, 1)), turn(kappa, 1))
    own = 1.0 - (west + east + up + down)
    edge_fixed = jnp.zeros(group, F32)
    for place, row in ((1, kappa[134:135]), (2, mask[134:135]), (4, kappa[0:1]), (5, mask[0:1])):
        edge_fixed = jnp.where(slot == place, row, edge_fixed)

    copies = []
    for name in range(2):
        fields[name].wait()
        for level in range(4):
            tilde = rows[level_rows(name, level)] * mask
            place = 2 + 4 * name + level
            field[place, centre] = tilde
            partial = (
                own * tilde
                + west * field[place, low]
                + east * field[place, high]
                + up * turn(tilde, -1)
                + down * turn(tilde, 1)
            )
            part[place, pl.ds(7, COLS)] = partial
            turned = lax.dot_general(
                chosen,
                part[place, 8:136].astype(BF16),
                (((1,), (1,)), ((), ())),
                preferred_element_type=F32,
            ).astype(BF16)
            others = jnp.where(slot == 0, partial[0:1], part[place, pl.ds(135, 8)])
            others = jnp.where(slot == 7, 0.0, others)
            edges = jnp.where(slot == 0, tilde[134:135], jnp.where(slot == 3, tilde[0:1], edge_fixed))
            others = spread(jnp.where(north, turn(others, 64), others))
            edges = spread(jnp.where(north, turn(edges, 64), edges))
            for quarter in range(4):
                place = chunk_row(16 * name + 4 * level + quarter, ORDER_OUT)
                chunks[place : place + ROWS] = turned[ROWS * quarter : ROWS * quarter + ROWS]
                two = [
                    jnp.sum(
                        jnp.where(in_slot, turn(value, -ROWS * quarter), 0.0), axis=0, keepdims=True
                    )
                    for value in (others, edges)
                ]
                chunks[place + ROWS : place + CHUNK] = jnp.concatenate(two, axis=0).astype(BF16)
            if level % 2:
                number = 2 * name + level // 2
                span = pl.ds(chunk_row(8 * number, ORDER_OUT), PART)
                copy = pltpu.make_async_copy(chunks.at[span], out_hbm.at[span], left.at[number])
                copy.start()
                copies.append(copy)
    for copy in copies:
        copy.wait()


def pack(adjoint, land, diffusivity):
    return pl.pallas_call(
        pack_kernel,
        out_shape=jax.ShapeDtypeStruct((RING * CHUNK, 128), BF16),
        in_specs=[pl.BlockSpec(memory_space=pl.ANY)] * 3,
        out_specs=pl.BlockSpec(memory_space=pl.ANY),
        scratch_shapes=[
            pltpu.VMEM((2 * FIELD, 128), F32),
            pltpu.VMEM((COLS, 128), jnp.int32),
            pltpu.VMEM((COLS, 2, 128), F32),
            pltpu.VMEM((10, 152, 128), F32),
            pltpu.VMEM((10, 144, 128), F32),
            pltpu.VMEM((RING * CHUNK, 128), BF16),
            pltpu.SemaphoreType.DMA((4,)),
            pltpu.SemaphoreType.DMA((4,)),
        ],
        compiler_params=pltpu.CompilerParams(vmem_limit_bytes=60 * 2**20),
        name="pack",
    )(adjoint, land, diffusivity)


def times(re, im, angle_index, count, sign):
    eighth = 8 * angle_index // count if 8 * angle_index % count == 0 else None
    half = math.sqrt(0.5)
    if eighth == 0:
        return re, im
    if eighth == 2:
        return (-im, re) if sign > 0 else (im, -re)
    if eighth == 1:
        if sign > 0:
            return half * (re - im), half * (re + im)
        return half * (re + im), half * (im - re)
    if eighth == 3:
        if sign > 0:
            return -half * (re + im), half * (re - im)
        return half * (im - re), -half * (re + im)
    cos = math.cos(2.0 * math.pi * angle_index / count)
    sin = sign * math.sin(2.0 * math.pi * angle_index / count)
    return cos * re - sin * im, sin * re + cos * im


def fourier(values):
    half = RING // 2
    while half:
        for start in range(0, RING, 2 * half):
            for i in range(half):
                a, b = start + i, start + i + half
                (ar, ai), (br, bi) = values[a], values[b]
                values[a] = (ar + br, ai + bi)
                values[b] = times(ar - br, ai - bi, i, 2 * half, -1)
        half //= 2


def fourier_back(values):
    half = 1
    while half < RING:
        for start in range(0, RING, 2 * half):
            for i in range(half):
                a, b = start + i, start + i + half
                ar, ai = values[a]
                br, bi = times(*values[b], i, 2 * half, 1)
                values[a] = (ar + br, ai + bi)
                values[b] = (ar - br, ai - bi)
        half *= 2


def ring_shift(value, step, columns):
    slot = lanes(value.shape) // ROWS
    for bit in range(5):
        moved = pltpu.roll(value, step * 2**bit % RING, 0)
        picked = jnp.zeros(value.shape, jnp.bool_)
        for place, column in enumerate(columns):
            if (column or 0) >> bit & 1:
                picked = jnp.logical_or(picked, slot == place)
        value = jnp.where(picked, moved, value)
    return value


def filter_kernel(*refs):
    @pl.when(at_pole())
    def _():
        filter_circles(*refs)


def filter_circles(
    in_ref, square_ref, forward_ref, backward_ref, inverse_ref, out_ref, held, wave, pair
):
    tile = (ROWS, 128)
    own_row = lanes(tile) % ROWS == sublanes(tile)
    column = lanes(tile) + 1
    rows = []
    for t in range(RING):
        start = chunk_row(INV * t % RING, ORDER_OUT)
        rows.append(in_ref[start : start + ROWS])
        pair[2 * t : 2 * t + 2] = in_ref[start + ROWS : start + CHUNK].astype(F32)
    for bit in range(5):
        picked = (column >> bit) & 1 == 1
        rows = [jnp.where(picked, rows[(t - 2**bit) % RING], rows[t]) for t in range(RING)]
    for t in range(RING):
        held[ROWS * t : ROWS * t + ROWS, 0:128] = rows[t]

    others, edges = pair[pl.ds(0, RING, stride=2)], pair[pl.ds(1, RING, stride=2)]
    slot = lanes(others.shape) // ROWS
    beyond = turn(pltpu.roll(edges, RING - 7, 0), -3 * ROWS)
    flux = (beyond - edges) * turn(0.5 * (beyond + edges), -ROWS) * turn(beyond * edges, -2 * ROWS)
    others = others + jnp.where(slot == 6, turn(flux, 6 * ROWS), 0.0)
    others = others - jnp.where(slot == 0, pltpu.roll(flux, 7, 0), 0.0)
    pair[0:RING] = ring_shift(others, 1, EXTRA)
    for t in range(RING):
        side = jnp.where(own_row, pair[t : t + 1], 0.0)
        held[ROWS * t : ROWS * t + ROWS, 128:256] = side.astype(BF16)

    wave[...] = jnp.dot(held[...], forward_ref[...], preferred_element_type=F32)
    for half in range(2):
        rows_of = [pl.ds(ROWS * t + 8 * half, 8) for t in range(RING)]
        values = [(wave[r, 0:128], wave[r, 128:256]) for r in rows_of]
        fourier(values)
        square = square_ref[8 * half : 8 * half + 8]
        for t in range(RING):
            keep = jnp.maximum(0.0, 1.0 - square * inverse_ref[t : t + 1]) * (1.0 / NLON)
            values[t] = (values[t][0] * keep, values[t][1] * keep)
        fourier_back(values)
        for t in range(RING):
            wave[rows_of[t], 0:128] = values[t][0]
            wave[rows_of[t], 128:256] = values[t][1]
    wave[...] = jnp.dot(wave[...].astype(BF16), backward_ref[...], preferred_element_type=F32)

    for t in range(RING):
        side = jnp.where(own_row, wave[ROWS * t : ROWS * t + ROWS, 128:256], 0.0)
        held[ROWS * t : ROWS * t + ROWS, 128:256] = side.astype(BF16)
    shape = (RING, RING * ROWS)
    gather = (lanes(shape) // ROWS == sublanes(shape)).astype(BF16)
    others = jnp.dot(gather, held[:, 128:256], preferred_element_type=F32)
    pair[0:RING] = ring_shift(others, -1, EXTRA[::-1])

    rows = [wave[ROWS * t : ROWS * t + ROWS, 0:128].astype(BF16) for t in range(RING)]
    for bit in range(5):
        picked = (column >> bit) & 1 == 1
        rows = [jnp.where(picked, rows[(t + 2**bit) % RING], rows[t]) for t in range(RING)]
    for d in range(RING):
        place = 7 * d % RING
        start = chunk_row(d, ORDER_BACK)
        out_ref[start : start + ROWS] = rows[place]
        last = jnp.broadcast_to(pair[place : place + 1], (2, 128))
        out_ref[start + ROWS : start + CHUNK] = last.astype(BF16)


def filter_rows(chunks, square):
    forward, backward, inverse_square = tables()
    return pl.pallas_call(
        filter_kernel,
        out_shape=jax.ShapeDtypeStruct((RING * CHUNK, 128), BF16),
        in_specs=[pl.BlockSpec(memory_space=pltpu.VMEM)] * 5,
        out_specs=pl.BlockSpec(memory_space=pltpu.VMEM),
        scratch_shapes=[
            pltpu.VMEM((RING * ROWS, 256), BF16),
            pltpu.VMEM((RING * ROWS, 256), F32),
            pltpu.VMEM((2 * RING, 128), F32),
        ],
        compiler_params=pltpu.CompilerParams(vmem_limit_bytes=24 * 2**20),
        name="filter",
    )(chunks, square, forward, backward, inverse_square)


def edge_kernel(adjoint_ref, land_ref, kappa_ref, near_ref, far_ref, side_ref, unfolded):
    lon_even = even("lon")
    whole = (COLS, 128)
    lane = lanes(whole)
    mask = land_ref[...].astype(F32)
    sides = jnp.zeros(whole, F32)
    near_ref[...] = jnp.zeros((24, 128), F32)
    far_ref[...] = jnp.zeros((24, 128), F32)
    for index in range(19):
        if index < 16:
            value = adjoint_ref[level_rows(index // 4, index % 4)] * mask
        elif index == 16:
            value = mask
        else:
            value = kappa_ref[:, index - 17, :]
        near_ref[index : index + 1] = jnp.where(lon_even, value[134:135], value[0:1])
        far_ref[index : index + 1] = jnp.where(lon_even, value[0:1], value[134:135])
        sides = jnp.where(lane // 2 == index, turn(value, 2 * index + 1), sides)
    unfolded[0:COLS] = sides
    lane = lanes((THIRD, 128))
    second, third = turn(unfolded[THIRD : 2 * THIRD], 40), turn(unfolded[2 * THIRD : 3 * THIRD], 80)
    side_ref[...] = jnp.where(
        lane < 40, unfolded[0:THIRD], jnp.where(lane < 80, second, third)
    )


def unfold(value):
    return jnp.concatenate([value, turn(value, -40), turn(value, -80)], axis=0)[0:COLS]


def edge(adjoint, land, diffusivity):
    return pl.pallas_call(
        edge_kernel,
        out_shape=(
            jax.ShapeDtypeStruct((24, 128), F32),
            jax.ShapeDtypeStruct((24, 128), F32),
            jax.ShapeDtypeStruct((THIRD, 128), F32),
        ),
        in_specs=[pl.BlockSpec(memory_space=pltpu.VMEM)] * 3,
        out_specs=[pl.BlockSpec(memory_space=pltpu.VMEM)] * 3,
        scratch_shapes=[pltpu.VMEM((3 * THIRD, 128), F32)],
        compiler_params=pltpu.CompilerParams(vmem_limit_bytes=24 * 2**20),
        name="edge",
    )(adjoint, land, diffusivity)


def stencil_kernel(
    adjoint_ref,
    land_ref,
    kappa_ref,
    near_side_ref,
    far_side_ref,
    out_ref,
    flow_ref,
    rim_ref,
    field,
):
    whole = (COLS, 128)
    lane = lanes(whole)
    centre, low, high = pl.ds(8, COLS), pl.ds(7, COLS), pl.ds(9, COLS)
    lat_even = even("lat")
    south_all = unfold(jnp.where(lat_even, far_side_ref[...], near_side_ref[...]))
    north_all = unfold(jnp.where(lat_even, near_side_ref[...], far_side_ref[...]))
    halos = jnp.where(lane % 2 == 0, south_all, turn(north_all, -2))
    mask = land_ref[...].astype(F32)
    clear_ends(field)

    def around(value, index):
        field[index, centre] = value
        halo = turn(halos, -2 * index)
        above = jnp.where(lane == 127, halo, turn(value, -1))
        below = jnp.where(lane == 0, halo, turn(value, 1))
        return field[index, low], field[index, high], above, below

    mask_around = around(mask, 16)
    weights = []
    for number in range(2):
        kappa = kappa_ref[:, number, :]
        near = around(kappa, 17 + number)
        four = [faces(mask, kappa, m, k) for m, k in zip(mask_around, near)]
        weights.append((1.0 - (four[0] + four[1] + four[2] + four[3]), *four))
    pressure_mask = PRESSURE * mask
    pressure_east, pressure_north = PRESSURE * mask_around[1], PRESSURE * mask_around[2]

    for level in range(4):
        density = None
        for name in range(4):
            own, *four = weights[name // 2]
            tilde = adjoint_ref[level_rows(name, level)] * mask
            near = around(tilde, 4 * name + level)
            total = own * tilde
            for weight, value in zip(four, near):
                total = total + weight * value
            if name == 0:
                density = pressure_east * tilde - pressure_mask * near[0]
            elif name == 1:
                density = density + pressure_north * tilde - pressure_mask * near[3]
            elif name == 2:
                total = total - ALPHA_T * density
            else:
                total = total + BETA_S * density
            if name < 2:
                flow_ref[level_rows(name, level)] = total
            else:
                out_ref[level_rows(name - 2, level)] = total
    for number, start in enumerate(RIM):
        rim_ref[8 * number : 8 * number + 8] = out_ref[start : start + 8]


def stencil(adjoint, land, diffusivity, near_side, far_side):
    return pl.pallas_call(
        stencil_kernel,
        grid=(1,),
        out_shape=(
            jax.ShapeDtypeStruct(adjoint.shape, F32),
            jax.ShapeDtypeStruct((2 * FIELD, 128), F32),
            jax.ShapeDtypeStruct((24, 128), F32),
        ),
        in_specs=[pl.BlockSpec(memory_space=pltpu.VMEM)] * 5,
        out_specs=[
            pl.BlockSpec((2 * FIELD, 128), lambda i: (1, 0)),
            pl.BlockSpec(memory_space=pltpu.VMEM),
            pl.BlockSpec(memory_space=pltpu.VMEM),
        ],
        scratch_shapes=[pltpu.VMEM((19, 152, 128), F32)],
        compiler_params=pltpu.CompilerParams(vmem_limit_bytes=24 * 2**20),
        name="stencil",
    )(adjoint, land, diffusivity, near_side, far_side)


def crossing(own_near, own_far, near, far):
    lon_even = even("lon")
    own_west, own_east = jnp.where(lon_even, own_far, own_near), jnp.where(lon_even, own_near, own_far)
    west, east = jnp.where(lon_even, far, near), jnp.where(lon_even, near, far)

    def flux(own, other):
        masks = own[16:17] * other[16:17]
        first, second = (0.5 * (own[k : k + 1] + other[k : k + 1]) * masks for k in (17, 18))
        step = other[0:16] - own[0:16]
        return first * step[0:8], second * step[8:16]

    west_flow, west_tracer = flux(own_west, west)
    east_flow, east_tracer = flux(own_east, east)
    west_density = -PRESSURE * own_west[16:17] * west[0:4]
    east_density = PRESSURE * east[16:17] * own_east[0:4]
    west_tracer += jnp.concatenate([-ALPHA_T * west_density, BETA_S * west_density], axis=0)
    east_tracer += jnp.concatenate([-ALPHA_T * east_density, BETA_S * east_density], axis=0)
    return west_flow, east_flow, west_tracer, east_tracer


def remove_kernel(
    chunks_ref,
    flow_ref,
    rim_ref,
    own_near_ref,
    own_far_ref,
    far_ref,
    near_ref,
    whole_ref,
    out_ref,
    new_flow,
    new_rim,
    high,
    done,
):
    del whole_ref
    west, east, west_tracer, east_tracer = crossing(
        own_near_ref[...], own_far_ref[...], near_ref[...], far_ref[...]
    )
    none = jnp.zeros((4, 128), F32)
    new_rim[...] = rim_ref[...] + jnp.concatenate(
        [west_tracer[0:4], none, east_tracer[0:4], west_tracer[4:8], none, east_tracer[4:8]], axis=0
    )
    copies = [
        pltpu.make_async_copy(
            new_rim.at[pl.ds(8 * number, 8)],
            out_ref.at[pl.ds(2 * FIELD + start, 8)],
            done.at[number],
        )
        for number, start in enumerate(RIM)
    ]
    polar = at_pole()
    for copy in copies:
        copy.start()
    for name, (start, size) in enumerate(((0, FIELD - 4), (FIELD - 4, FIELD + 4))):

        @pl.when(polar)
        def _():
            remove_waves(name, chunks_ref, flow_ref, new_flow, high)

        rows = pl.ds(FIELD * name, FIELD)

        @pl.when(jnp.logical_not(polar))
        def _():
            new_flow[rows] = flow_ref[rows]

        first, last = pl.ds(FIELD * name, 4), pl.ds(FIELD * name + FIELD - 4, 4)
        new_flow[first] = new_flow[first] + west[4 * name : 4 * name + 4]
        new_flow[last] = new_flow[last] + east[4 * name : 4 * name + 4]
        rows = pl.ds(start, size)
        copy = pltpu.make_async_copy(new_flow.at[rows], out_ref.at[rows], done.at[3 + name])
        copy.start()
        copies.append(copy)
    for copy in copies:
        copy.wait()


def remove_waves(name, chunks_ref, flow_ref, out_ref, high):
    north = poles()[1]
    group, square = (8, 128), (128, 128)
    quarter_of = (lanes(group) // ROWS + sublanes(group)) % 8
    here = (lanes(square) >= 64) == north
    for level in range(0, 4, 2):
        first = 16 * name + 4 * level
        starts = [chunk_row(first + place, ORDER_BACK) for place in range(8)]
        both = jnp.concatenate([chunks_ref[a : a + ROWS].astype(F32) for a in starts], axis=0).T
        across = turn(both, 64)
        for second in range(2):
            others = jnp.zeros(group, F32)
            for quarter in range(4):
                start = starts[4 * second + quarter] + ROWS
                row = turn(chunks_ref[start : start + 2].astype(F32)[0:1], ROWS * (quarter + 1))
                others = jnp.where(quarter_of == quarter, row, others)
            others = spread(others)
            others = jnp.where(north, turn(others, 64), others)
            straight = jnp.where(north, across, both) if second == 0 else jnp.where(north, both, across)
            place = level + second
            high[place, 1:129] = jnp.where(here, straight, 0.0)
            high[place, 0:1] = others[0:1]
            high[place, 129:135] = others[1:7]
            rows_of = level_rows(name, place)
            out_ref[rows_of] = flow_ref[rows_of] - high[place, 0:COLS]


def remove(chunks, flow, rim, own_near, own_far, far, near, whole):
    return pl.pallas_call(
        remove_kernel,
        out_shape=jax.ShapeDtypeStruct(whole.shape, F32),
        in_specs=[pl.BlockSpec(memory_space=pltpu.VMEM)] * 7 + [pl.BlockSpec(memory_space=pl.ANY)],
        out_specs=pl.BlockSpec(memory_space=pl.ANY),
        scratch_shapes=[
            pltpu.VMEM((2 * FIELD, 128), F32),
            pltpu.VMEM((24, 128), F32),
            pltpu.VMEM((4, 136, 128), F32),
            pltpu.SemaphoreType.DMA((5,)),
        ],
        input_output_aliases={7: 0},
        compiler_params=pltpu.CompilerParams(vmem_limit_bytes=24 * 2**20),
        name="remove",
    )(chunks, flow, rim, own_near, own_far, far, near, whole)


def swap(value, axis, first):
    count = lax.axis_size(axis)
    pairs = []
    for a in range(first, count, 2):
        b = a + 1
        if b == count:
            if axis == "lat":
                continue
            b = 0
        pairs += [(a, b), (b, a)]
    return lax.ppermute(value, axis, pairs)


def exchange(chunks, order):
    pairs = chunks.reshape(-1, 2, chunks.shape[1])
    return lax.all_to_all(
        pairs, "lon", split_axis=0, concat_axis=0, axis_index_groups=[order], tiled=True
    ).reshape(chunks.shape)


def local(adjoint, land, diffusivity, cutoff):
    lon_index, lat_index = lax.axis_index("lon"), lax.axis_index("lat")
    first_cut = jnp.where(lat_index == lax.axis_size("lat") - 1, PROWS, 0) + lon_index % 4 * ROWS
    cuts = lax.dynamic_slice_in_dim(cutoff, first_cut, ROWS, 0)
    square = jnp.broadcast_to(jnp.square(cuts.astype(F32))[:, None], (ROWS, 128))

    shape = adjoint.shape
    fields = jnp.transpose(adjoint, (0, 2, 1, 3)).reshape(-1, shape[3])
    kappas = jnp.transpose(diffusivity, (1, 0, 2))

    circles = exchange(pack(fields, land, kappas), ORDER_OUT)
    own_near, own_far, sides = edge(fields, land, kappas)
    far_side = swap(sides, "lat", 1)
    near_side = swap(sides, "lat", 0)
    circles, near_side, far_side = lax.optimization_barrier((circles, near_side, far_side))

    filtered = filter_rows(circles, square)
    filtered, own_near, own_far = lax.optimization_barrier((filtered, own_near, own_far))
    removed = exchange(filtered, ORDER_BACK)
    far = swap(own_far, "lon", 1)
    near = swap(own_near, "lon", 0)
    whole, flow, rim = stencil(fields, land, kappas, near_side, far_side)

    out = remove(removed, flow, rim, own_near, own_far, far, near, whole)
    return jnp.transpose(out.reshape(shape[0], shape[2], shape[1], shape[3]), (0, 2, 1, 3))


def solution(mesh):
    placed = (P(None, None, "lon", "lat"), P("lon", "lat"), P(None, "lon", "lat"), P())
    return jax.shard_map(
        local, mesh=mesh, in_specs=placed, out_specs=P(None, None, "lon", "lat"), check_vma=False
    )
```

```python
import math

import jax
import jax.numpy as jnp
import numpy as np
from jax import lax
from jax.experimental import pallas as pl
from jax.experimental.pallas import tpu as pltpu
from jax.sharding import PartitionSpec as P

PROWS = 64
PRESSURE = 0.3
ALPHA_T = 1.0
BETA_S = 0.8

RING = 32
COLS = 135
NLON = RING * COLS
INV = 23
CRT_RING = 3105
CRT_COLS = 1216
ORDER_OUT = [((place + 24) % RING) ^ 1 for place in range(RING)]
ORDER_BACK = [17] + [tile for tile in reversed(range(RING)) if tile != 17]
WAVES = 68
ROWS = 16
LEVELS = 4
FIELD = COLS * LEVELS
RIM = (0, FIELD - 4, 2 * FIELD - 8)
CHUNK = ROWS + 2
THIRD = 48
PART = 8 * CHUNK

MAIN = [lane + 1 for lane in range(128)]
EXTRA = [0] + list(range(129, 135)) + [None]

F32 = jnp.float32
BF16 = jnp.bfloat16


def tables():
    waves = np.arange(WAVES)

    def transform(slots):
        columns = MAIN + [column for column in slots for _ in range(ROWS)]
        used = np.array([[float(column is not None)] for column in columns])
        order = np.array([[column or 0] for column in columns])
        angle = 2.0 * math.pi * ((38 * order * waves) % COLS) / COLS
        table = np.zeros((256, 256))
        table[:, :WAVES] = np.cos(angle) * used
        table[:, 128 : 128 + WAVES] = -np.sin(angle) * used
        return table

    forward, backward = transform(EXTRA), transform(EXTRA[::-1]).T
    backward *= np.where(np.arange(256) % 128 == 0, 1.0, 2.0)[:, None]
    inverse_square = np.ones((RING, 128))
    for place in range(RING):
        kappa = int(format(place, "05b")[::-1], 2)
        ring_wave = 7 * kappa % RING
        k = (CRT_RING * ring_wave + CRT_COLS * waves) % NLON
        k = np.minimum(k, NLON - k)
        inverse_square[place, :WAVES] = np.where(k == 0, 1e6, 1.0 / np.maximum(k, 1) ** 2)
    return (
        jnp.asarray(forward, BF16),
        jnp.asarray(backward, BF16),
        jnp.asarray(inverse_square, F32),
    )


def chunk_row(tile, order):
    return CHUNK * order.index(tile)


def turn(value, shift):
    size = value.shape[-1]
    shift %= size
    return value if shift == 0 else pltpu.roll(value, shift, value.ndim - 1)


def lanes(shape):
    return lax.broadcasted_iota(jnp.int32, shape, len(shape) - 1)


def sublanes(shape):
    return lax.broadcasted_iota(jnp.int32, shape, len(shape) - 2)


def level_rows(field, level):
    return pl.ds(FIELD * field + level, COLS, stride=LEVELS)


def faces(mask, kappa, mask_near, kappa_near):
    return 0.5 * (kappa + kappa_near) * mask * mask_near


def poles():
    index = lax.axis_index("lat")
    return index == 0, index == lax.axis_size("lat") - 1


def at_pole():
    south, north = poles()
    return jnp.logical_or(south, north)


def even(axis):
    return lax.axis_index(axis) % 2 == 0


def clear_ends(field):
    for place in range(field.shape[0]):
        field[place, 0:8] = jnp.zeros((8, 128), F32)
        field[place, 136:144] = jnp.zeros((8, 128), F32)


def spread(value):
    return pltpu.roll(value, 0, 1, stride=ROWS, stride_axis=0)


def pack_kernel(*refs):
    @pl.when(at_pole())
    def _():
        pack_rows(*refs)


def pack_rows(
    adjoint_hbm, land_hbm, kappa_hbm, out_hbm, rows, land, kappas, field, part, chunks, arrived, left
):
    def arrival(source, target, number):
        copy = pltpu.make_async_copy(source, target, arrived.at[number])
        copy.start()
        return copy

    first = arrival(land_hbm, land, 0), arrival(kappa_hbm, kappas, 1)
    half = FIELD + 4
    fields = [
        arrival(adjoint_hbm.at[pl.ds(start, size)], rows.at[pl.ds(start, size)], number)
        for number, start, size in ((2, 0, half), (3, half, 2 * FIELD - half))
    ]
    north = poles()[1]
    whole = (COLS, 128)
    low, high = pl.ds(7, COLS), pl.ds(9, COLS)
    centre = pl.ds(8, COLS)
    clear_ends(field)
    lane = lanes(whole)
    chosen = (lanes((PROWS, 128)) == sublanes((PROWS, 128)) + jnp.where(north, 64, 0)).astype(BF16)
    group = (8, 128)
    slot = sublanes(group)
    in_slot = lanes(group) // ROWS == slot

    for copy in first:
        copy.wait()
    mask = land[...].astype(F32)
    kappa = kappas[:, 0, :]
    field[0, centre] = kappa
    kappa_west, kappa_east = field[0, low], field[0, high]
    field[1, centre] = mask
    mask_west, mask_east = field[1, low], field[1, high]
    west = faces(mask, kappa, mask_west, kappa_west)
    east = faces(mask, kappa, mask_east, kappa_east)
    up = faces(mask, kappa, jnp.where(lane == 127, 0.0, turn(mask, -1)), turn(kappa, -1))
    down = faces(mask, kappa, jnp.where(lane == 0, 0.0, turn(mask, 1)), turn(kappa, 1))
    own = 1.0 - (west + east + up + down)
    edge_fixed = jnp.zeros(group, F32)
    for place, row in ((1, kappa[134:135]), (2, mask[134:135]), (4, kappa[0:1]), (5, mask[0:1])):
        edge_fixed = jnp.where(slot == place, row, edge_fixed)

    copies = []
    for name in range(2):
        fields[name].wait()
        for level in range(4):
            tilde = rows[level_rows(name, level)] * mask
            place = 2 + 4 * name + level
            field[place, centre] = tilde
            partial = (
                own * tilde
                + west * field[place, low]
                + east * field[place, high]
                + up * turn(tilde, -1)
                + down * turn(tilde, 1)
            )
            part[place, pl.ds(7, COLS)] = partial
            turned = lax.dot_general(
                chosen,
                part[place, 8:136].astype(BF16),
                (((1,), (1,)), ((), ())),
                preferred_element_type=F32,
            ).astype(BF16)
            others = jnp.where(slot == 0, partial[0:1], part[place, pl.ds(135, 8)])
            others = jnp.where(slot == 7, 0.0, others)
            edges = jnp.where(slot == 0, tilde[134:135], jnp.where(slot == 3, tilde[0:1], edge_fixed))
            others = spread(jnp.where(north, turn(others, 64), others))
            edges = spread(jnp.where(north, turn(edges, 64), edges))
            for quarter in range(4):
                place = chunk_row(16 * name + 4 * level + quarter, ORDER_OUT)
                chunks[place : place + ROWS] = turned[ROWS * quarter : ROWS * quarter + ROWS]
                two = [
                    jnp.sum(
                        jnp.where(in_slot, turn(value, -ROWS * quarter), 0.0), axis=0, keepdims=True
                    )
                    for value in (others, edges)
                ]
                chunks[place + ROWS : place + CHUNK] = jnp.concatenate(two, axis=0).astype(BF16)
            if level % 2:
                number = 2 * name + level // 2
                span = pl.ds(PART * (ORDER_OUT.index(8 * number) // 8), PART)
                copy = pltpu.make_async_copy(chunks.at[span], out_hbm.at[span], left.at[number])
                copy.start()
                copies.append(copy)
    for copy in copies:
        copy.wait()


def pack(adjoint, land, diffusivity):
    return pl.pallas_call(
        pack_kernel,
        out_shape=jax.ShapeDtypeStruct((RING * CHUNK, 128), BF16),
        in_specs=[pl.BlockSpec(memory_space=pl.ANY)] * 3,
        out_specs=pl.BlockSpec(memory_space=pl.ANY),
        scratch_shapes=[
            pltpu.VMEM((2 * FIELD, 128), F32),
            pltpu.VMEM((COLS, 128), jnp.int32),
            pltpu.VMEM((COLS, 2, 128), F32),
            pltpu.VMEM((10, 152, 128), F32),
            pltpu.VMEM((10, 144, 128), F32),
            pltpu.VMEM((RING * CHUNK, 128), BF16),
            pltpu.SemaphoreType.DMA((4,)),
            pltpu.SemaphoreType.DMA((4,)),
        ],
        compiler_params=pltpu.CompilerParams(vmem_limit_bytes=60 * 2**20),
        name="pack",
    )(adjoint, land, diffusivity)


def times(re, im, angle_index, count, sign):
    eighth = 8 * angle_index // count if 8 * angle_index % count == 0 else None
    half = math.sqrt(0.5)
    if eighth == 0:
        return re, im
    if eighth == 2:
        return (-im, re) if sign > 0 else (im, -re)
    if eighth == 1:
        if sign > 0:
            return half * (re - im), half * (re + im)
        return half * (re + im), half * (im - re)
    if eighth == 3:
        if sign > 0:
            return -half * (re + im), half * (re - im)
        return half * (im - re), -half * (re + im)
    cos = math.cos(2.0 * math.pi * angle_index / count)
    sin = sign * math.sin(2.0 * math.pi * angle_index / count)
    return cos * re - sin * im, sin * re + cos * im


def fourier(values):
    half = RING // 2
    while half:
        for start in range(0, RING, 2 * half):
            for i in range(half):
                a, b = start + i, start + i + half
                (ar, ai), (br, bi) = values[a], values[b]
                values[a] = (ar + br, ai + bi)
                values[b] = times(ar - br, ai - bi, i, 2 * half, -1)
        half //= 2


def fourier_back(values):
    half = 1
    while half < RING:
        for start in range(0, RING, 2 * half):
            for i in range(half):
                a, b = start + i, start + i + half
                ar, ai = values[a]
                br, bi = times(*values[b], i, 2 * half, 1)
                values[a] = (ar + br, ai + bi)
                values[b] = (ar - br, ai - bi)
        half *= 2


def ring_shift(value, step, columns):
    slot = lanes(value.shape) // ROWS
    for bit in range(5):
        moved = pltpu.roll(value, step * 2**bit % RING, 0)
        picked = jnp.zeros(value.shape, jnp.bool_)
        for place, column in enumerate(columns):
            if (column or 0) >> bit & 1:
                picked = jnp.logical_or(picked, slot == place)
        value = jnp.where(picked, moved, value)
    return value


def filter_kernel(*refs):
    @pl.when(at_pole())
    def _():
        filter_circles(*refs)


def filter_circles(
    in_ref, square_ref, forward_ref, backward_ref, inverse_ref, out_ref, held, wave, pair
):
    tile = (ROWS, 128)
    own_row = lanes(tile) % ROWS == sublanes(tile)
    column = lanes(tile) + 1
    rows = []
    for t in range(RING):
        start = chunk_row(INV * t % RING, ORDER_OUT)
        rows.append(in_ref[start : start + ROWS])
        pair[2 * t : 2 * t + 2] = in_ref[start + ROWS : start + CHUNK].astype(F32)
    for bit in range(5):
        picked = (column >> bit) & 1 == 1
        rows = [jnp.where(picked, rows[(t - 2**bit) % RING], rows[t]) for t in range(RING)]
    for t in range(RING):
        held[ROWS * t : ROWS * t + ROWS, 0:128] = rows[t]

    others, edges = pair[pl.ds(0, RING, stride=2)], pair[pl.ds(1, RING, stride=2)]
    slot = lanes(others.shape) // ROWS
    beyond = turn(pltpu.roll(edges, RING - 7, 0), -3 * ROWS)
    flux = (beyond - edges) * turn(0.5 * (beyond + edges), -ROWS) * turn(beyond * edges, -2 * ROWS)
    others = others + jnp.where(slot == 6, turn(flux, 6 * ROWS), 0.0)
    others = others - jnp.where(slot == 0, pltpu.roll(flux, 7, 0), 0.0)
    pair[0:RING] = ring_shift(others, 1, EXTRA)
    for t in range(RING):
        side = jnp.where(own_row, pair[t : t + 1], 0.0)
        held[ROWS * t : ROWS * t + ROWS, 128:256] = side.astype(BF16)

    wave[...] = jnp.dot(held[...], forward_ref[...], preferred_element_type=F32)
    for half in range(2):
        rows_of = [pl.ds(ROWS * t + 8 * half, 8) for t in range(RING)]
        values = [(wave[r, 0:128], wave[r, 128:256]) for r in rows_of]
        fourier(values)
        square = square_ref[8 * half : 8 * half + 8]
        for t in range(RING):
            keep = jnp.maximum(0.0, 1.0 - square * inverse_ref[t : t + 1]) * (1.0 / NLON)
            values[t] = (values[t][0] * keep, values[t][1] * keep)
        fourier_back(values)
        for t in range(RING):
            wave[rows_of[t], 0:128] = values[t][0]
            wave[rows_of[t], 128:256] = values[t][1]
    wave[...] = jnp.dot(wave[...].astype(BF16), backward_ref[...], preferred_element_type=F32)

    for t in range(RING):
        side = jnp.where(own_row, wave[ROWS * t : ROWS * t + ROWS, 128:256], 0.0)
        held[ROWS * t : ROWS * t + ROWS, 128:256] = side.astype(BF16)
    shape = (RING, RING * ROWS)
    gather = (lanes(shape) // ROWS == sublanes(shape)).astype(BF16)
    others = jnp.dot(gather, held[:, 128:256], preferred_element_type=F32)
    pair[0:RING] = ring_shift(others, -1, EXTRA[::-1])

    rows = [wave[ROWS * t : ROWS * t + ROWS, 0:128].astype(BF16) for t in range(RING)]
    for bit in range(5):
        picked = (column >> bit) & 1 == 1
        rows = [jnp.where(picked, rows[(t + 2**bit) % RING], rows[t]) for t in range(RING)]
    for d in range(RING):
        place = 7 * d % RING
        start = chunk_row(d, ORDER_BACK)
        out_ref[start : start + ROWS] = rows[place]
        last = jnp.broadcast_to(pair[place : place + 1], (2, 128))
        out_ref[start + ROWS : start + CHUNK] = last.astype(BF16)


def filter_rows(chunks, square):
    forward, backward, inverse_square = tables()
    return pl.pallas_call(
        filter_kernel,
        out_shape=jax.ShapeDtypeStruct((RING * CHUNK, 128), BF16),
        in_specs=[pl.BlockSpec(memory_space=pltpu.VMEM)] * 5,
        out_specs=pl.BlockSpec(memory_space=pltpu.VMEM),
        scratch_shapes=[
            pltpu.VMEM((RING * ROWS, 256), BF16),
            pltpu.VMEM((RING * ROWS, 256), F32),
            pltpu.VMEM((2 * RING, 128), F32),
        ],
        compiler_params=pltpu.CompilerParams(vmem_limit_bytes=24 * 2**20),
        name="filter",
    )(chunks, square, forward, backward, inverse_square)


def edge_kernel(adjoint_ref, land_ref, kappa_ref, near_ref, far_ref, side_ref, unfolded):
    lon_even = even("lon")
    whole = (COLS, 128)
    lane = lanes(whole)
    mask = land_ref[...].astype(F32)
    sides = jnp.zeros(whole, F32)
    near_ref[...] = jnp.zeros((24, 128), F32)
    far_ref[...] = jnp.zeros((24, 128), F32)
    for index in range(19):
        if index < 16:
            value = adjoint_ref[level_rows(index // 4, index % 4)] * mask
        elif index == 16:
            value = mask
        else:
            value = kappa_ref[:, index - 17, :]
        near_ref[index : index + 1] = jnp.where(lon_even, value[134:135], value[0:1])
        far_ref[index : index + 1] = jnp.where(lon_even, value[0:1], value[134:135])
        sides = jnp.where(lane // 2 == index, turn(value, 2 * index + 1), sides)
    unfolded[0:COLS] = sides
    lane = lanes((THIRD, 128))
    second, third = turn(unfolded[THIRD : 2 * THIRD], 40), turn(unfolded[2 * THIRD : 3 * THIRD], 80)
    side_ref[...] = jnp.where(
        lane < 40, unfolded[0:THIRD], jnp.where(lane < 80, second, third)
    )


def unfold(value):
    return jnp.concatenate([value, turn(value, -40), turn(value, -80)], axis=0)[0:COLS]


def edge(adjoint, land, diffusivity):
    return pl.pallas_call(
        edge_kernel,
        out_shape=(
            jax.ShapeDtypeStruct((24, 128), F32),
            jax.ShapeDtypeStruct((24, 128), F32),
            jax.ShapeDtypeStruct((THIRD, 128), F32),
        ),
        in_specs=[pl.BlockSpec(memory_space=pltpu.VMEM)] * 3,
        out_specs=[pl.BlockSpec(memory_space=pltpu.VMEM)] * 3,
        scratch_shapes=[pltpu.VMEM((3 * THIRD, 128), F32)],
        compiler_params=pltpu.CompilerParams(vmem_limit_bytes=24 * 2**20),
        name="edge",
    )(adjoint, land, diffusivity)


def stencil_kernel(
    adjoint_ref,
    land_ref,
    kappa_ref,
    near_side_ref,
    far_side_ref,
    out_ref,
    flow_ref,
    rim_ref,
    field,
):
    whole = (COLS, 128)
    lane = lanes(whole)
    centre, low, high = pl.ds(8, COLS), pl.ds(7, COLS), pl.ds(9, COLS)
    lat_even = even("lat")
    south_all = unfold(jnp.where(lat_even, far_side_ref[...], near_side_ref[...]))
    north_all = unfold(jnp.where(lat_even, near_side_ref[...], far_side_ref[...]))
    halos = jnp.where(lane % 2 == 0, south_all, turn(north_all, -2))
    mask = land_ref[...].astype(F32)
    clear_ends(field)

    def around(value, index):
        field[index, centre] = value
        halo = turn(halos, -2 * index)
        above = jnp.where(lane == 127, halo, turn(value, -1))
        below = jnp.where(lane == 0, halo, turn(value, 1))
        return field[index, low], field[index, high], above, below

    mask_around = around(mask, 16)
    weights = []
    for number in range(2):
        kappa = kappa_ref[:, number, :]
        near = around(kappa, 17 + number)
        four = [faces(mask, kappa, m, k) for m, k in zip(mask_around, near)]
        weights.append((1.0 - (four[0] + four[1] + four[2] + four[3]), *four))
    pressure_mask = PRESSURE * mask
    pressure_east, pressure_north = PRESSURE * mask_around[1], PRESSURE * mask_around[2]

    for level in range(4):
        density = None
        for name in range(4):
            own, *four = weights[name // 2]
            tilde = adjoint_ref[level_rows(name, level)] * mask
            near = around(tilde, 4 * name + level)
            total = own * tilde
            for weight, value in zip(four, near):
                total = total + weight * value
            if name == 0:
                density = pressure_east * tilde - pressure_mask * near[0]
            elif name == 1:
                density = density + pressure_north * tilde - pressure_mask * near[3]
            elif name == 2:
                total = total - ALPHA_T * density
            else:
                total = total + BETA_S * density
            if name < 2:
                flow_ref[level_rows(name, level)] = total
            else:
                out_ref[level_rows(name - 2, level)] = total
    for number, start in enumerate(RIM):
        rim_ref[8 * number : 8 * number + 8] = out_ref[start : start + 8]


def stencil(adjoint, land, diffusivity, near_side, far_side):
    return pl.pallas_call(
        stencil_kernel,
        grid=(1,),
        out_shape=(
            jax.ShapeDtypeStruct(adjoint.shape, F32),
            jax.ShapeDtypeStruct((2 * FIELD, 128), F32),
            jax.ShapeDtypeStruct((24, 128), F32),
        ),
        in_specs=[pl.BlockSpec(memory_space=pltpu.VMEM)] * 5,
        out_specs=[
            pl.BlockSpec((2 * FIELD, 128), lambda i: (1, 0)),
            pl.BlockSpec(memory_space=pltpu.VMEM),
            pl.BlockSpec(memory_space=pltpu.VMEM),
        ],
        scratch_shapes=[pltpu.VMEM((19, 152, 128), F32)],
        compiler_params=pltpu.CompilerParams(vmem_limit_bytes=24 * 2**20),
        name="stencil",
    )(adjoint, land, diffusivity, near_side, far_side)


def crossing(own_near, own_far, near, far):
    lon_even = even("lon")
    own_west, own_east = jnp.where(lon_even, own_far, own_near), jnp.where(lon_even, own_near, own_far)
    west, east = jnp.where(lon_even, far, near), jnp.where(lon_even, near, far)

    def flux(own, other):
        masks = own[16:17] * other[16:17]
        first, second = (0.5 * (own[k : k + 1] + other[k : k + 1]) * masks for k in (17, 18))
        step = other[0:16] - own[0:16]
        return first * step[0:8], second * step[8:16]

    west_flow, west_tracer = flux(own_west, west)
    east_flow, east_tracer = flux(own_east, east)
    west_density = -PRESSURE * own_west[16:17] * west[0:4]
    east_density = PRESSURE * east[16:17] * own_east[0:4]
    west_tracer += jnp.concatenate([-ALPHA_T * west_density, BETA_S * west_density], axis=0)
    east_tracer += jnp.concatenate([-ALPHA_T * east_density, BETA_S * east_density], axis=0)
    return west_flow, east_flow, west_tracer, east_tracer


def remove_kernel(
    chunks_ref,
    flow_ref,
    rim_ref,
    own_near_ref,
    own_far_ref,
    far_ref,
    near_ref,
    whole_ref,
    out_ref,
    new_flow,
    new_rim,
    high,
    done,
):
    del whole_ref
    west, east, west_tracer, east_tracer = crossing(
        own_near_ref[...], own_far_ref[...], near_ref[...], far_ref[...]
    )
    none = jnp.zeros((4, 128), F32)
    new_rim[...] = rim_ref[...] + jnp.concatenate(
        [west_tracer[0:4], none, east_tracer[0:4], west_tracer[4:8], none, east_tracer[4:8]], axis=0
    )
    copies = [
        pltpu.make_async_copy(
            new_rim.at[pl.ds(8 * number, 8)],
            out_ref.at[pl.ds(2 * FIELD + start, 8)],
            done.at[number],
        )
        for number, start in enumerate(RIM)
    ]
    polar = at_pole()
    for copy in copies:
        copy.start()
    for name, (start, size) in enumerate(((0, FIELD - 4), (FIELD - 4, FIELD + 4))):

        @pl.when(polar)
        def _():
            remove_waves(name, chunks_ref, flow_ref, new_flow, high)

        rows = pl.ds(FIELD * name, FIELD)

        @pl.when(jnp.logical_not(polar))
        def _():
            new_flow[rows] = flow_ref[rows]

        first, last = pl.ds(FIELD * name, 4), pl.ds(FIELD * name + FIELD - 4, 4)
        new_flow[first] = new_flow[first] + west[4 * name : 4 * name + 4]
        new_flow[last] = new_flow[last] + east[4 * name : 4 * name + 4]
        rows = pl.ds(start, size)
        copy = pltpu.make_async_copy(new_flow.at[rows], out_ref.at[rows], done.at[3 + name])
        copy.start()
        copies.append(copy)
    for copy in copies:
        copy.wait()


def remove_waves(name, chunks_ref, flow_ref, out_ref, high):
    north = poles()[1]
    group, square = (8, 128), (128, 128)
    quarter_of = (lanes(group) // ROWS + sublanes(group)) % 8
    here = (lanes(square) >= 64) == north
    for level in range(0, 4, 2):
        first = 16 * name + 4 * level
        starts = [chunk_row(first + place, ORDER_BACK) for place in range(8)]
        both = jnp.concatenate([chunks_ref[a : a + ROWS].astype(F32) for a in starts], axis=0).T
        across = turn(both, 64)
        for second in range(2):
            others = jnp.zeros(group, F32)
            for quarter in range(4):
                start = starts[4 * second + quarter] + ROWS
                row = turn(chunks_ref[start : start + 2].astype(F32)[0:1], ROWS * (quarter + 1))
                others = jnp.where(quarter_of == quarter, row, others)
            others = spread(others)
            others = jnp.where(north, turn(others, 64), others)
            straight = jnp.where(north, across, both) if second == 0 else jnp.where(north, both, across)
            place = level + second
            high[place, 1:129] = jnp.where(here, straight, 0.0)
            high[place, 0:1] = others[0:1]
            high[place, 129:135] = others[1:7]
            rows_of = level_rows(name, place)
            out_ref[rows_of] = flow_ref[rows_of] - high[place, 0:COLS]


def remove(chunks, flow, rim, own_near, own_far, far, near, whole):
    return pl.pallas_call(
        remove_kernel,
        out_shape=jax.ShapeDtypeStruct(whole.shape, F32),
        in_specs=[pl.BlockSpec(memory_space=pltpu.VMEM)] * 7 + [pl.BlockSpec(memory_space=pl.ANY)],
        out_specs=pl.BlockSpec(memory_space=pl.ANY),
        scratch_shapes=[
            pltpu.VMEM((2 * FIELD, 128), F32),
            pltpu.VMEM((24, 128), F32),
            pltpu.VMEM((4, 136, 128), F32),
            pltpu.SemaphoreType.DMA((5,)),
        ],
        input_output_aliases={7: 0},
        compiler_params=pltpu.CompilerParams(vmem_limit_bytes=24 * 2**20),
        name="remove",
    )(chunks, flow, rim, own_near, own_far, far, near, whole)


def swap(value, axis, first):
    count = lax.axis_size(axis)
    pairs = []
    for a in range(first, count, 2):
        b = a + 1
        if b == count:
            if axis == "lat":
                continue
            b = 0
        pairs += [(a, b), (b, a)]
    return lax.ppermute(value, axis, pairs)


def exchange(chunks, order):
    pairs = chunks.reshape(-1, 2, chunks.shape[1])
    return lax.all_to_all(
        pairs, "lon", split_axis=0, concat_axis=0, axis_index_groups=[order], tiled=True
    ).reshape(chunks.shape)


def local(adjoint, land, diffusivity, cutoff):
    lon_index, lat_index = lax.axis_index("lon"), lax.axis_index("lat")
    first_cut = jnp.where(lat_index == lax.axis_size("lat") - 1, PROWS, 0) + lon_index % 4 * ROWS
    cuts = lax.dynamic_slice_in_dim(cutoff, first_cut, ROWS, 0)
    square = jnp.broadcast_to(jnp.square(cuts.astype(F32))[:, None], (ROWS, 128))

    shape = adjoint.shape
    fields = jnp.transpose(adjoint, (0, 2, 1, 3)).reshape(-1, shape[3])
    kappas = jnp.transpose(diffusivity, (1, 0, 2))

    circles = exchange(pack(fields, land, kappas), ORDER_OUT)
    own_near, own_far, sides = edge(fields, land, kappas)
    far_side = swap(sides, "lat", 1)
    near_side = swap(sides, "lat", 0)
    circles, near_side, far_side = lax.optimization_barrier((circles, near_side, far_side))

    filtered = filter_rows(circles, square)
    filtered, own_near, own_far = lax.optimization_barrier((filtered, own_near, own_far))
    removed = exchange(filtered, ORDER_BACK)
    far = swap(own_far, "lon", 1)
    near = swap(own_near, "lon", 0)
    whole, flow, rim = stencil(fields, land, kappas, near_side, far_side)

    out = remove(removed, flow, rim, own_near, own_far, far, near, whole)
    return jnp.transpose(out.reshape(shape[0], shape[2], shape[1], shape[3]), (0, 2, 1, 3))


def solution(mesh):
    placed = (P(None, None, "lon", "lat"), P("lon", "lat"), P(None, "lon", "lat"), P())
    return jax.shard_map(
        local, mesh=mesh, in_specs=placed, out_specs=P(None, None, "lon", "lat"), check_vma=False
    )
```
